512 devices in a mesh: dp: 32 (over z, core), expert: 16 (over x, y).
Axes of the slice: x: 4, y: 4, z: 16, core: 2. Of those that a mesh axis runs over, the one named last changes fastest.
Arguments:
- tokens: bfloat16 [6144, 2560], P(('dp', 'expert')), may hold values from -6 to 6
- norm_scale_vector: float32 [2560], replicated, may hold values from 0.5 to 1.5
- router: bfloat16 [2560, 16], replicated, may hold values from -0.125 to 0.125
- routes: int32 [6144], P(('dp', 'expert')), may hold values from 0 to 15, as said below
- session_speaker: int32 [6144], P(('dp', 'expert')), may hold values from 0 to 31, as said below
- adapter_slots: int32 [16, 32], P('expert'), may hold values from 0 to 31, each once within a row
- speaker_down_weight: bfloat16 [16, 32, 64, 2560], P('expert', 'dp'), may hold values from -0.125 to 0.125
- speaker_up_weight: bfloat16 [16, 32, 64, 2560], P('expert', 'dp'), may hold values from -0.75 to 0.75
- routed_gate_weight: bfloat16 [16, 2560, 4096], P('expert', None, 'dp'), may hold values from -0.125 to 0.125
- routed_up_weight: bfloat16 [16, 2560, 4096], P('expert', None, 'dp'), may hold values from -0.125 to 0.125
- routed_down_weight: bfloat16 [16, 4096, 2560], P('expert', 'dp'), may hold values from -0.09375 to 0.09375
- common_gate_weight: bfloat16 [2560, 4096], P(None, 'dp'), may hold values from -0.125 to 0.125
- common_up_weight: bfloat16 [2560, 4096], P(None, 'dp'), may hold values from -0.125 to 0.125
- common_down_weight: bfloat16 [4096, 2560], P('dp'), may hold values from -0.09375 to 0.09375
Outputs:
- mixed: bfloat16 [6144, 2560], P(('dp', 'expert'))
The draws below stay inside these ranges and needn't reach their ends.
Inputs may be any that keep to these rules, and one draw needn't show every extreme that they name: `routes`: among the sessions of one device no expert is named more than 2 times, and some expert exactly 2 times; among the sessions of one index of dp (16 devices) no expert is named more than 13 times, and some expert exactly 13 times. `session_speaker`: the sessions of one device all name different adapters. `adapter_slots`: each row is a permutation.
All inputs are finite; a program needn't handle non-finite values.
Results may differ from the reference program's by a relative error of at most 0.014.
Values may be sent and summed in bfloat16 or wider, within the bound.
A program may use at most 64 MiB of HBM per device.

```python
import jax
import jax.numpy as jnp
from jax import lax

HIDDEN_WIDTH = 2560
FF = 4096
FS = 4096
ADAPTER_RANK = 64
EXPERTS = 16
SESSIONS_LOCAL = 12
REPLICA_GROUP = 16
EXPERT_GROUP = 32
ADAPTERS_LOCAL = 1
BUCKET = 13
SESSION_TOTAL = 6144


def draw_routes(key, part):
    key = jax.random.fold_in(key, 11)
    perm_key, turn_key, shuffle_key = jax.random.split(key, 3)
    member_ids = lax.broadcasted_iota(jnp.int32, (REPLICA_GROUP, SESSIONS_LOCAL), 0)
    session_ids = lax.broadcasted_iota(jnp.int32, (REPLICA_GROUP, SESSIONS_LOCAL), 1)
    stream = (member_ids * SESSIONS_LOCAL + session_ids) % EXPERTS
    stream = jnp.where((member_ids == 0) & (session_ids == 1), 0, stream).astype(jnp.int32)
    perm_keys = jax.random.split(perm_key, EXPERT_GROUP)
    orders_of_experts = jax.vmap(lambda one_key: jax.random.permutation(one_key, EXPERTS))(perm_keys).astype(jnp.int32)
    turns = jax.random.randint(turn_key, (EXPERT_GROUP,), 0, REPLICA_GROUP).astype(jnp.int32)
    rotated = (jnp.arange(REPLICA_GROUP, dtype=jnp.int32)[None, :] - turns[:, None]) % REPLICA_GROUP
    picked = stream[rotated]
    named = jax.vmap(lambda table, where: table[where])(orders_of_experts, picked)
    shuffle_keys = jax.random.split(shuffle_key, EXPERT_GROUP * REPLICA_GROUP)
    shuffles = jax.vmap(lambda one_key: jax.random.permutation(one_key, SESSIONS_LOCAL))(shuffle_keys).astype(jnp.int32)
    shuffles = shuffles.reshape(EXPERT_GROUP, REPLICA_GROUP, SESSIONS_LOCAL)
    shuffled = jnp.take_along_axis(named, shuffles, axis=2)
    return shuffled.reshape(-1).astype(jnp.int32)


def draw_session_speaker(key, part):
    key = jax.random.fold_in(key, 23)
    liking_key, jitter_key = jax.random.split(key)
    stored = EXPERT_GROUP * ADAPTERS_LOCAL
    liking = jax.random.randint(liking_key, (REPLICA_GROUP, stored), 0, 4).astype(jnp.int32)
    jitter_values = jax.random.randint(jitter_key, (EXPERT_GROUP, REPLICA_GROUP, stored), 0, 65536).astype(jnp.int32)
    scores = (liking[None, :, :] * 65536 + jitter_values) * stored + jnp.arange(stored, dtype=jnp.int32)
    _, picked = lax.top_k(scores, SESSIONS_LOCAL)
    return picked.reshape(-1).astype(jnp.int32)


def steps_of(key, dims, shards, least, largest):
    def one(dim, shards_of):
        draws = jax.random.uniform(jax.random.fold_in(jax.random.fold_in(key, 6), dim), (shards_of,), jnp.float32, least / len(shards), largest / len(shards))
        return jnp.repeat(jnp.exp(draws), dims[dim] // shards_of).reshape((-1,) + (1,) * (len(dims) - dim - 1))

    loudness = one(*shards[0])
    for cut in shards[1:]:
        loudness = loudness * one(*cut)
    return loudness


def bell_draw(key, extent, spread, most, cuts=(), kind=jnp.bfloat16):
    values = jax.random.normal(key, extent, jnp.float32) * spread
    if len(cuts) > 0:
        values = steps_of(key, extent, cuts, -0.22, 0.18) * values
    return jnp.clip(values, min=-most, max=most).astype(kind)


def setup_inputs(seed: int = 0) -> dict:
    seeds = jax.random.split(jax.random.key(seed), 15)
    tokens = bell_draw(seeds[0], (SESSION_TOTAL, HIDDEN_WIDTH), 1.0, 6.0, ((0, 512),))
    norm_scale_vector = jnp.clip(1.0 + 0.1 * jax.random.normal(seeds[1], (HIDDEN_WIDTH,), jnp.float32), 0.5, 1.5)
    router = bell_draw(seeds[2], (HIDDEN_WIDTH, EXPERTS), HIDDEN_WIDTH ** -0.5, 0.125)
    routes = draw_routes(jax.random.fold_in(seeds[14], 71), 0)
    session_speaker = draw_session_speaker(jax.random.fold_in(seeds[14], 71), 0)
    adapter_slots = jax.vmap(lambda own: jax.random.permutation(own, EXPERT_GROUP * ADAPTERS_LOCAL))(jax.random.split(seeds[5], REPLICA_GROUP)).reshape((REPLICA_GROUP, EXPERT_GROUP * ADAPTERS_LOCAL)).astype(jnp.int32)
    speaker_down_weight = bell_draw(seeds[6], (REPLICA_GROUP, EXPERT_GROUP * ADAPTERS_LOCAL, ADAPTER_RANK, HIDDEN_WIDTH), HIDDEN_WIDTH ** -0.5, 0.125, ((0, 16), (1, 32)))
    speaker_up_weight = bell_draw(seeds[7], (REPLICA_GROUP, EXPERT_GROUP * ADAPTERS_LOCAL, ADAPTER_RANK, HIDDEN_WIDTH), ADAPTER_RANK ** -0.5, 0.75, ((0, 16), (1, 32)))
    routed_gate_weight = bell_draw(seeds[8], (EXPERTS, HIDDEN_WIDTH, FF), HIDDEN_WIDTH ** -0.5, 0.125, ((0, 16), (2, 32)))
    routed_up_weight = bell_draw(seeds[9], (EXPERTS, HIDDEN_WIDTH, FF), HIDDEN_WIDTH ** -0.5, 0.125, ((0, 16), (2, 32)))
    routed_down_weight = bell_draw(seeds[10], (EXPERTS, FF, HIDDEN_WIDTH), FF ** -0.5, 0.09375, ((0, 16), (1, 32)))
    common_gate_weight = bell_draw(seeds[11], (HIDDEN_WIDTH, FS), HIDDEN_WIDTH ** -0.5, 0.125, ((1, 32),))
    common_up_weight = bell_draw(seeds[12], (HIDDEN_WIDTH, FS), HIDDEN_WIDTH ** -0.5, 0.125, ((1, 32),))
    common_down_weight = bell_draw(seeds[13], (FS, HIDDEN_WIDTH), FS ** -0.5, 0.09375, ((0, 32),))
    return {"tokens": tokens, "norm_scale_vector": norm_scale_vector, "router": router, "routes": routes, "session_speaker": session_speaker, "adapter_slots": adapter_slots, "speaker_down_weight": speaker_down_weight, "speaker_up_weight": speaker_up_weight, "routed_gate_weight": routed_gate_weight, "routed_up_weight": routed_up_weight, "routed_down_weight": routed_down_weight, "common_gate_weight": common_gate_weight, "common_up_weight": common_up_weight, "common_down_weight": common_down_weight}


norm_eps = 1e-05

def swiglu(rows_in, gate_weight, up_weight):
    gate_part = jnp.dot(rows_in, gate_weight, preferred_element_type=jnp.float32)
    up_part = jnp.dot(rows_in, up_weight, preferred_element_type=jnp.float32)
    return (jax.nn.silu(gate_part) * up_part).astype(jnp.bfloat16)

def blocked_down(hidden, down_weight):
    block_width = down_weight.shape[0] // EXPERT_GROUP

    def add_block(index, running):
        begin = (index * block_width).astype(jnp.int32)
        hidden_block = lax.dynamic_slice_in_dim(hidden, begin, block_width, 1)
        down_block = lax.dynamic_slice_in_dim(down_weight, begin, block_width, 0)
        partial_value = jnp.dot(hidden_block, down_block, preferred_element_type=jnp.float32)
        rounded = lax.optimization_barrier(partial_value.astype(jnp.bfloat16))
        return running + rounded.astype(jnp.float32)
    start_value = jnp.zeros((hidden.shape[0], down_weight.shape[1]), jnp.float32)
    return lax.fori_loop(0, EXPERT_GROUP, add_block, start_value)

def reference(tokens, norm_scale_vector, router, routes, session_speaker, adapter_slots, speaker_down_weight, speaker_up_weight, routed_gate_weight, routed_up_weight, routed_down_weight, common_gate_weight, common_up_weight, common_down_weight):
    expanded_tokens = tokens.astype(jnp.float32)
    scale_rows = lax.rsqrt(lax.optimization_barrier(jnp.mean(expanded_tokens * expanded_tokens, axis=-1, keepdims=True)) + norm_eps)
    normed = (expanded_tokens * scale_rows * norm_scale_vector).astype(jnp.bfloat16)
    logits = jnp.dot(normed, router, preferred_element_type=jnp.float32)
    gate_probability = jax.nn.sigmoid(jnp.take_along_axis(logits, routes[:, None], axis=1)[:, 0])
    common_output = blocked_down(swiglu(normed, common_gate_weight, common_up_weight), common_down_weight)
    capacity_rows = EXPERT_GROUP * BUCKET

    def one_expert(running, packed):
        gate_weight, up_weight, down_weight, expert_index = packed
        row_order = jnp.argsort((routes != expert_index).astype(jnp.int32), stable=True)[:capacity_rows]
        belongs = routes[row_order] == expert_index
        summed = blocked_down(swiglu(normed[row_order], gate_weight, up_weight), down_weight)
        result = lax.optimization_barrier(summed.astype(jnp.bfloat16)).astype(jnp.float32)
        return (running.at[row_order].add(jnp.where(belongs[:, None], result, 0.0)), None)
    routed_start = jnp.zeros((SESSION_TOTAL, HIDDEN_WIDTH), jnp.float32)
    expert_numbers = jnp.arange(EXPERTS, dtype=jnp.int32)
    dispatched_tokens, _ = lax.scan(one_expert, routed_start, (routed_gate_weight, routed_up_weight, routed_down_weight, expert_numbers))
    column_major = normed.reshape(EXPERT_GROUP, REPLICA_GROUP, SESSIONS_LOCAL, HIDDEN_WIDTH).transpose(1, 0, 2, 3).reshape(REPLICA_GROUP, EXPERT_GROUP * SESSIONS_LOCAL, HIDDEN_WIDTH)
    adapters = session_speaker.reshape(EXPERT_GROUP, REPLICA_GROUP, SESSIONS_LOCAL).transpose(1, 0, 2).reshape(REPLICA_GROUP, EXPERT_GROUP * SESSIONS_LOCAL)
    slot_buffer = jnp.take_along_axis(adapter_slots, adapters, axis=1)

    def single_column(packed):
        column_rows, column_storage, down_all, up_all = packed
        chosen_down = down_all[column_storage].astype(jnp.float32)
        chosen_up = up_all[column_storage].astype(jnp.float32)
        reduced_hidden = jnp.einsum('rd,rkd->rk', column_rows.astype(jnp.float32), chosen_down).astype(jnp.bfloat16)
        return jnp.einsum('rk,rkd->rd', reduced_hidden.astype(jnp.float32), chosen_up).astype(jnp.bfloat16)
    adapter_updates = lax.map(single_column, (column_major, slot_buffer, speaker_down_weight, speaker_up_weight))
    speaker_update = adapter_updates.reshape(REPLICA_GROUP, EXPERT_GROUP, SESSIONS_LOCAL, HIDDEN_WIDTH).transpose(1, 0, 2, 3).reshape(SESSION_TOTAL, HIDDEN_WIDTH)
    mixed = expanded_tokens + common_output + gate_probability[:, None] * dispatched_tokens + speaker_update.astype(jnp.float32)
    return mixed.astype(jnp.bfloat16)
```

```python
import functools

import jax
import jax.numpy as jnp
from jax import lax
from jax.experimental import pallas as pl
from jax.experimental.pallas import tpu as pltpu
from jax.sharding import PartitionSpec as P

SLOTS = 2
MESH = pl.DeviceIdType.MESH
BF = jnp.bfloat16
F32 = jnp.float32
norm_eps = 1e-05
ROWS = 16
CHUNKS = 2


def moe_kernel(
    planes,
    rows_ref,
    router_ref,
    cg_ref,
    rg_ref,
    cu_ref,
    ru_ref,
    cd_ref,
    rd_ref,
    out_ref,
    gath,
    w1,
    w2,
    hid,
    part,
    first,
    recv,
    own_sem,
    wsend,
    wrecv,
    gsend,
    grecv,
    rsend,
    rrecv,
):
    dp = lax.axis_index("dp")
    col = lax.axis_index("expert")
    z = dp // 2
    core = lax.rem(dp, 2)
    width = rows_ref.shape[1]
    part_width = width // CHUNKS
    half = cg_ref.shape[2]
    up_dev = (lax.rem(z + 1, planes) * 2 + core, col)
    down_dev = (lax.rem(z + planes - 1, planes) * 2 + core, col)
    sibling = (z * 2 + 1 - core, col)

    sources = (cg_ref, rg_ref, cu_ref, ru_ref)
    own = []
    for j in range(4):
        own.append(pltpu.make_async_copy(sources[j].at[0], w1.at[j, :, pl.ds(0, half)], own_sem.at[j]))
    for j, ref in enumerate((cd_ref, rd_ref)):
        own.append(
            pltpu.make_async_copy(ref.at[0], w2.at[pl.ds(2 * j * half, half)], own_sem.at[4 + j])
        )
    for copy in own:
        copy.start()

    barrier = pltpu.get_barrier_semaphore()
    for peer in (up_dev, down_dev, sibling):
        pl.semaphore_signal(barrier, inc=1, device_id=peer, device_id_type=MESH)
    gath[z] = rows_ref[...]
    pl.semaphore_wait(barrier, 3)

    def length(d, ch):
        return planes // 2 if (ch < CHUNKS // 2) == (d == 0) else planes // 2 - 1

    sends = []
    last = {}
    for step in range(planes // 2 + 1):
        for ch in range(CHUNKS):
            for d in range(2):
                if step > 0 and step <= length(d, ch):
                    last[d, ch].wait_recv()
                if step >= length(d, ch):
                    continue
                src = lax.rem(z + (planes - step if d == 0 else step), planes)
                piece = gath.at[src, :, pl.ds(ch * part_width, part_width)]
                copy = pltpu.make_async_remote_copy(
                    piece,
                    piece,
                    gsend.at[d, step, ch],
                    grecv.at[d, step, ch],
                    device_id=up_dev if d == 0 else down_dev,
                    device_id_type=MESH,
                )
                copy.start()
                sends.append(copy)
                last[d, ch] = copy
        if step == 0:
            weights = []
            for j in range(4):
                weights.append((sources[j].at[0], w1.at[j, :, pl.ds(half, half)]))
            for j, ref in enumerate((cd_ref, rd_ref)):
                weights.append((ref.at[0], w2.at[pl.ds((2 * j + 1) * half, half)]))
            shared = []
            for j, (src_ref, dst_ref) in enumerate(weights):
                copy = pltpu.make_async_remote_copy(
                    src_ref,
                    dst_ref,
                    wsend.at[j],
                    wrecv.at[j],
                    device_id=sibling,
                    device_id_type=MESH,
                )
                copy.start()
                shared.append(copy)
    for copy in own:
        copy.wait()
    for copy in shared:
        copy.wait()
    for copy in sends:
        copy.wait_send()

    total = planes * ROWS
    rows = gath[...].reshape(total, width)
    logits = jnp.dot(rows, router_ref[...], preferred_element_type=F32)
    lane = lax.broadcasted_iota(jnp.int32, logits.shape, 1)
    chosen = jnp.sum(jnp.where(lane == col, logits, 0.0), axis=1, keepdims=True)
    gate_prob = 1.0 / (1.0 + jnp.exp(-chosen))
    for n in range(2):
        gate = jnp.dot(rows, w1[n], preferred_element_type=F32)
        up = jnp.dot(rows, w1[2 + n], preferred_element_type=F32)
        value = gate / (1.0 + jnp.exp(-gate)) * up
        if n == 1:
            value = value * gate_prob
        hid[:, pl.ds(2 * n * half, 2 * half)] = value.astype(BF)

    @pl.loop(0, width // 256)
    def _(t):
        cols = pl.ds(pl.multiple_of(t * 256, 256), 256)
        product = jnp.dot(hid[...], w2[:, cols], preferred_element_type=F32)
        part[:, :, cols] = product.reshape(planes, ROWS, 256)

    sends = []
    last = {}
    for step in range(planes // 2 + 1):
        for ch in range(CHUNKS):
            for d in range(2):
                n = length(d, ch)
                if step > n:
                    continue
                cols = pl.ds(ch * part_width, part_width)
                if step > 0:
                    last[d, ch].wait_recv()
                if step == n:
                    continue
                dest = lax.rem(z + (n - step if d == 0 else planes - n + step), planes)
                if step == 0:
                    block = first.at[d, :, cols]
                    block[...] = part[dest, :, cols].astype(BF)
                else:
                    block = recv.at[d, step - 1, :, cols]
                    block[...] = (block[...].astype(F32) + part[dest, :, cols]).astype(BF)
                copy = pltpu.make_async_remote_copy(
                    block,
                    recv.at[d, step, :, cols],
                    rsend.at[d, step, ch],
                    rrecv.at[d, step, ch],
                    device_id=up_dev if d == 0 else down_dev,
                    device_id_type=MESH,
                )
                copy.start()
                sends.append(copy)
                last[d, ch] = copy
    for ch in range(CHUNKS):
        cols = pl.ds(ch * part_width, part_width)
        value = part[z, :, cols]
        for d in range(2):
            value = value + recv[d, length(d, ch) - 1, :, cols].astype(F32)
        out_ref[:, cols] = value.astype(BF)
    for copy in sends:
        copy.wait_send()


def moe_call(rows, router, cg, rg, cu, ru, cd, rd):
    planes = lax.axis_size("dp") // 2
    width = rows.shape[1]
    half = cg.shape[2]
    vmem = pl.BlockSpec(memory_space=pltpu.VMEM)
    hbm = pl.BlockSpec(memory_space=pl.ANY)
    dma = pltpu.SemaphoreType.DMA
    steps = planes // 2
    return pl.pallas_call(
        functools.partial(moe_kernel, planes),
        out_shape=jax.ShapeDtypeStruct((ROWS, width), BF),
        in_specs=[vmem, vmem] + [hbm] * 6,
        out_specs=vmem,
        scratch_shapes=[
            pltpu.VMEM((planes, ROWS, width), BF),
            pltpu.VMEM((4, width, 2 * half), BF),
            pltpu.VMEM((4 * half, width), BF),
            pltpu.VMEM((planes * ROWS, 4 * half), BF),
            pltpu.VMEM((planes, ROWS, width), F32),
            pltpu.VMEM((2, ROWS, width), BF),
            pltpu.VMEM((2, steps, ROWS, width), BF),
            dma((6,)),
            dma((6,)),
            dma((6,)),
            dma((2, steps, CHUNKS)),
            dma((2, steps, CHUNKS)),
            dma((2, steps, CHUNKS)),
            dma((2, steps, CHUNKS)),
        ],
        compiler_params=pltpu.CompilerParams(
            collective_id=1, has_side_effects=True, vmem_limit_bytes=56 * 1024 * 1024
        ),
    )(rows, router, cg, rg, cu, ru, cd, rd)


def body(
    tokens,
    norm_scale_vector,
    router,
    routes,
    session_speaker,
    adapter_slots,
    speaker_down_weight,
    speaker_up_weight,
    routed_gate_weight,
    routed_up_weight,
    routed_down_weight,
    common_gate_weight,
    common_up_weight,
    common_down_weight,
):
    sessions = tokens.shape[0]
    model_width = tokens.shape[1]
    members = lax.axis_size("expert")
    owners = lax.axis_size("dp")
    experts = router.shape[1]
    bucket = ROWS
    expanded_tokens = tokens.astype(jnp.float32)
    scale_rows = lax.rsqrt(
        jnp.mean(expanded_tokens * expanded_tokens, axis=-1, keepdims=True) + norm_eps
    )
    normed = (expanded_tokens * scale_rows * norm_scale_vector).astype(jnp.bfloat16)
    later_index = lax.broadcasted_iota(jnp.int32, (sessions, sessions), 0)
    earlier_index = lax.broadcasted_iota(jnp.int32, (sessions, sessions), 1)
    same_route = (routes[:, None] == routes[None, :]) & (earlier_index < later_index)
    slot_rank = jnp.sum(same_route.astype(jnp.int32), axis=1)
    slot_index = routes * SLOTS + slot_rank
    placing = (
        lax.broadcasted_iota(jnp.int32, (experts * SLOTS, sessions), 0) == slot_index[None, :]
    ).astype(jnp.bfloat16)
    send_rows = jnp.dot(placing, normed, preferred_element_type=jnp.float32).astype(jnp.bfloat16)
    send_rows = send_rows.reshape(members, SLOTS, model_width)
    send_flags = jnp.sum(placing, axis=1).reshape(members, SLOTS)
    got_rows, got_flags = (
        lax.all_to_all(send_rows, "expert", split_axis=0, concat_axis=0, tiled=True),
        lax.all_to_all(send_flags, "expert", split_axis=0, concat_axis=0, tiled=True),
    )
    arrived_flags = got_flags.astype(jnp.int32).reshape(1, members * SLOTS)
    before_count = jnp.cumsum(arrived_flags, axis=1) - arrived_flags
    bucket_ids = lax.broadcasted_iota(jnp.int32, (bucket, members * SLOTS), 0)
    packing = ((arrived_flags == 1) & (before_count == bucket_ids)).astype(jnp.bfloat16)
    compact = jnp.dot(
        packing,
        got_rows.reshape(members * SLOTS, model_width),
        preferred_element_type=jnp.float32,
    ).astype(jnp.bfloat16)
    routed_back = moe_call(
        compact,
        router,
        common_gate_weight[None],
        routed_gate_weight,
        common_up_weight[None],
        routed_up_weight,
        common_down_weight[None],
        routed_down_weight,
    )
    returning = jnp.dot(packing.T, routed_back, preferred_element_type=jnp.float32).astype(
        jnp.bfloat16
    )
    returning = returning.reshape(members, SLOTS, model_width)
    home_rows = lax.all_to_all(
        returning, "expert", split_axis=0, concat_axis=0, tiled=True
    ).reshape(experts * SLOTS, model_width)
    local_dispatched = jnp.dot(placing.T, home_rows, preferred_element_type=jnp.float32)
    adapter_ids = lax.broadcasted_iota(jnp.int32, (sessions, owners), 1)
    owner_of = jnp.sum(
        jnp.where(session_speaker[:, None] == adapter_ids, adapter_slots[0][None, :], 0), axis=1
    )
    outbound_tokens = (
        lax.broadcasted_iota(jnp.int32, (owners, sessions), 0) == owner_of[None, :]
    ).astype(jnp.bfloat16)
    outgoing = jnp.dot(outbound_tokens, normed, preferred_element_type=jnp.float32).astype(
        jnp.bfloat16
    )
    outgoing = outgoing.reshape(owners, 1, model_width)
    received_tokens = lax.all_to_all(outgoing, "dp", split_axis=0, concat_axis=0, tiled=True)
    reduced_hidden = jnp.einsum(
        "fnw,nvw->fnv", received_tokens, speaker_down_weight[0], preferred_element_type=jnp.float32
    ).astype(jnp.bfloat16)
    adapter_delta = jnp.einsum(
        "snu,nut->snt", reduced_hidden, speaker_up_weight[0], preferred_element_type=jnp.float32
    ).astype(jnp.bfloat16)
    gathered_back = lax.all_to_all(
        adapter_delta, "dp", split_axis=0, concat_axis=0, tiled=True
    ).reshape(owners, model_width)
    speaker_rows = jnp.dot(outbound_tokens.T, gathered_back, preferred_element_type=jnp.float32)
    mixed = expanded_tokens + local_dispatched + speaker_rows
    return mixed.astype(jnp.bfloat16)


def solution(mesh):
    in_specs = (
        P(("dp", "expert"), None),
        P(),
        P(),
        P(("dp", "expert")),
        P(("dp", "expert")),
        P("expert", None),
        P("expert", "dp", None, None),
        P("expert", "dp", None, None),
        P("expert", None, "dp"),
        P("expert", None, "dp"),
        P("expert", "dp", None),
        P(None, "dp"),
        P(None, "dp"),
        P("dp", None),
    )
    out_specs = P(("dp", "expert"), None)
    return jax.shard_map(body, mesh=mesh, in_specs=in_specs, out_specs=out_specs, check_vma=False)
```

```python
import functools

import jax
import jax.numpy as jnp
from jax import lax
from jax.experimental import pallas as pl
from jax.experimental.pallas import tpu as pltpu
from jax.sharding import PartitionSpec as P

MESH = pl.DeviceIdType.MESH
BF = jnp.bfloat16
F32 = jnp.float32
I32 = jnp.int32
norm_eps = 1e-05
ROWS = 16
LANES = 128
PACK = 8


def iota(shape, dim):
    return lax.broadcasted_iota(I32, shape, dim)


def one_hot(condition):
    return jnp.where(condition, 1.0, 0.0).astype(BF)


def stack(rows, fill):
    tiles = rows.shape[1] // LANES
    columns = []
    for t in range(-(-tiles // PACK)):
        pieces = []
        for j in range(PACK):
            i = t * PACK + j
            if i < tiles:
                pieces.append(rows[:, i * LANES : (i + 1) * LANES])
            else:
                pieces.append(jnp.full((ROWS, LANES), fill if i == tiles else 0.0, rows.dtype))
        columns.append(jnp.concatenate(pieces, axis=0))
    return jnp.concatenate(columns, axis=1)


def tile_of(stacked, i):
    t, j = i // PACK, i % PACK
    return stacked[j * ROWS : (j + 1) * ROWS, t * LANES : (t + 1) * LANES]


def unstack(stacked, tiles):
    return jnp.concatenate([tile_of(stacked, i) for i in range(tiles)], axis=1)


def dot(a, b):
    return jnp.dot(a, b, preferred_element_type=F32)


def dot_t(a, b):
    return lax.dot_general(a, b, (((0,), (0,)), ((), ())), preferred_element_type=F32)


def dot_nt(a, b):
    return lax.dot_general(a, b, (((1,), (1,)), ((), ())), preferred_element_type=F32)


def block_kernel(
    planes,
    columns,
    routes_ref,
    speaker_ref,
    slots_ref,
    tokens_ref,
    gain_ref,
    router_ref,
    cg_ref,
    rg_ref,
    cu_ref,
    ru_ref,
    cd_ref,
    rd_ref,
    down_ref,
    up_ref,
    out_ref,
    tok,
    w1,
    w2,
    wd,
    wu,
    xs,
    xr,
    ls,
    lr,
    lr2,
    rs,
    rr,
    bs,
    br,
    br2,
    pack_ref,
    gath,
    hid,
    pb,
    first,
    rb,
    ystage,
    yb,
    own_sem,
    wsem,
    xsem,
    lsem,
    rsem,
    bsem,
    exsem,
    blksem,
    gsem,
    dsem,
    psem,
    qsem,
    ysem,
):
    dp = lax.axis_index("dp")
    col = lax.axis_index("expert")
    z = dp // 2
    core = lax.rem(dp, 2)
    sessions, width = tokens_ref.shape
    tiles = width // LANES
    half = cg_ref.shape[2]
    hops = planes // 2
    side = width // 2
    sibling = (z * 2 + 1 - core, col)

    def plane(offset):
        return lax.rem(z + offset, planes)

    def remote(src, dst, sem, index, device):
        return pltpu.make_async_remote_copy(
            src,
            dst,
            sem.at[(0, *index)],
            sem.at[(1, *index)],
            device_id=device,
            device_id_type=MESH,
        )

    sources = (cg_ref, rg_ref, cu_ref, ru_ref)
    own = []
    for j in range(4):
        own.append(
            pltpu.make_async_copy(sources[j].at[0], w1.at[j, :, pl.ds(0, half)], own_sem.at[j])
        )
    for j, ref in enumerate((cd_ref, rd_ref)):
        own.append(
            pltpu.make_async_copy(ref.at[0], w2.at[pl.ds(2 * j * half, half)], own_sem.at[4 + j])
        )
    own.append(pltpu.make_async_copy(down_ref.at[0, 0], wd, own_sem.at[6]))
    own.append(pltpu.make_async_copy(up_ref.at[0, 0], wu, own_sem.at[7]))
    for copy in own:
        copy.start()

    barrier = pltpu.get_barrier_semaphore()
    pl.semaphore_signal(barrier, inc=1, device_id=sibling, device_id_type=MESH)

    def greet_plane(d, carry):
        pl.semaphore_signal(
            barrier, inc=1, device_id=(plane(d) * 2 + core, col), device_id_type=MESH
        )
        return carry

    def greet_column(d, carry):
        pl.semaphore_signal(
            barrier, inc=1, device_id=(dp, lax.rem(col + d, columns)), device_id_type=MESH
        )
        return carry

    lax.fori_loop(1, planes, greet_plane, 0)
    lax.fori_loop(1, columns, greet_column, 0)

    tok[...] = jnp.zeros_like(tok)
    tok[0:sessions, :] = tokens_ref[...].astype(F32)
    x = tok[...]
    scale = lax.rsqrt(jnp.mean(x * x, axis=-1, keepdims=True) + norm_eps)
    normed = (x * scale * gain_ref[...]).astype(BF)

    routes = [routes_ref[s] for s in range(sessions)]
    route_slot = []
    for s in range(sessions):
        rank = jnp.int32(0)
        for earlier in range(s):
            rank = rank + jnp.where(routes[earlier] == routes[s], 1, 0)
        route_slot.append(routes[s] * 2 + rank)
    storage = [slots_ref[0, speaker_ref[s]] for s in range(sessions)]

    def spread(values, index):
        held = jnp.full(index.shape, -1, I32)
        for s in range(sessions):
            held = jnp.where(index == s, values[s], held)
        return held

    pairs = 2 * PACK
    outer = columns * pairs
    inner = PACK * ROWS
    row = iota((outer, inner), 0)
    lane = iota((outer, inner), 1)
    lane_session = jnp.bitwise_and(iota((1, inner), 1), ROWS - 1)
    same_piece = jnp.bitwise_and(row, PACK - 1) == lane // ROWS
    stacked = stack(normed, 1.0)
    to_expert = one_hot(same_piece & (row // PACK == spread(route_slot, lane_session)))
    xs[...] = dot(to_expert, stacked).astype(BF).reshape(xs.shape)
    to_adapter = one_hot(same_piece & (row // PACK == spread(storage, lane_session)))
    ls[...] = dot(to_adapter, stacked).astype(BF).reshape(ls.shape)

    pl.semaphore_wait(barrier, planes + columns - 1)

    def over_columns(src, dst, sem, d):
        to = lax.rem(col + d, columns)
        return remote(src.at[to], dst.at[col], sem, (d,), (dp, to))

    def over_planes(src, dst, sem, d):
        to = plane(d)
        return remote(src.at[to], dst.at[z], sem, (d,), (to * 2 + core, col))

    def start_all(over, src, dst, sem, count):
        def step(d, carry):
            over(src, dst, sem, d).start()
            return carry

        lax.fori_loop(1, count, step, 0)

    def wait_all(over, src, dst, sem, count):
        def step(d, carry):
            over(src, dst, sem, d).wait()
            return carry

        lax.fori_loop(1, count, step, 0)

    start_all(over_columns, xs, xr, xsem, columns)
    xr[col] = xs[col]
    start_all(over_planes, ls, lr, lsem, planes)
    lr[z] = ls[z]

    shared = []
    for j in range(4):
        shared.append(
            remote(sources[j].at[0], w1.at[j, :, pl.ds(half, half)], wsem, (j,), sibling)
        )
    for j, ref in enumerate((cd_ref, rd_ref)):
        shared.append(
            remote(ref.at[0], w2.at[pl.ds((2 * j + 1) * half, half)], wsem, (4 + j,), sibling)
        )
    for copy in shared:
        copy.start()

    wait_all(over_columns, xs, xr, xsem, columns)
    arrived = xr[...].reshape(outer, 3 * LANES)
    flags = jnp.where(
        jnp.bitwise_and(row, PACK - 1) == tiles % PACK, arrived[:, 2 * LANES :], 0.0
    ).astype(BF)
    left = iota((outer, outer), 0) // PACK
    right = iota((outer, outer), 1) // PACK
    before = dot_t(flags, one_hot(left < right))
    taken = dot_t(flags, one_hot(left == right))
    wide_row = iota((inner, outer), 0)
    wide_lane = iota((inner, outer), 1)
    wide_piece = wide_row // ROWS == jnp.bitwise_and(wide_lane, PACK - 1)
    wide_index = jnp.bitwise_and(wide_row, ROWS - 1)
    pack_ref[...] = one_hot(
        wide_piece & (taken > 0.5) & (jnp.abs(before - wide_index.astype(F32)) < 0.5)
    )
    gath[core, z] = unstack(dot(pack_ref[...], arrived).astype(BF), tiles)

    def pick(half_index):
        return one_hot(
            wide_piece
            & (wide_index == wide_lane // pairs)
            & (jnp.bitwise_and(wide_lane // PACK, 1) == half_index)
        )

    def adapter_meet():
        wait_all(over_planes, ls, lr, lsem, planes)
        remote(lr, lr2, exsem, (0,), sibling).start()

    def adapter_apply():
        remote(lr, lr2, exsem, (0,), sibling).wait()
        for copy in own[6:]:
            copy.wait()
        mine, other = pick(core), pick(1 - core)
        parts = []
        for buffer in (lr, lr2):
            parts.append(unstack(dot(mine, buffer[...].reshape(outer, -1)).astype(BF), tiles))
        low = dot_nt(jnp.concatenate(parts, axis=0), wd[...]).astype(BF)
        delta = dot(low, wu[...]).astype(BF)
        back = dot_t(mine, stack(delta[:ROWS], 0.0)) + dot_t(other, stack(delta[ROWS:], 0.0))
        bs[...] = back.astype(BF).reshape(bs.shape)
        start_all(over_planes, bs, br, bsem, planes)
        br[z] = bs[z]

    def length(d, part):
        return hops if part == d else hops - 1

    near = ((plane(1) * 2 + core, col), (plane(planes - 1) * 2 + core, col))

    def from_plane(d, step):
        return plane(planes - step if d == 0 else step)

    def gather_copy(d, step, h, part):
        piece = gath.at[h, from_plane(d, step), :, pl.ds(part * side, side)]
        return remote(piece, piece, gsem, (d, step, h, part), near[d])

    def hand_over(d, step, part):
        piece = gath.at[0, from_plane(d, step), :, pl.ds(part * side, side)]
        return remote(piece, piece, dsem, (d, step, part), sibling)

    block_copy = remote(gath.at[0, z], gath.at[0, z], blksem, (), sibling)

    @pl.when(core == 1)
    def _():
        for h in (1, 0):
            if h == 0:
                block_copy.wait_recv()
            for part in range(2):
                for d in range(2):
                    gather_copy(d, 0, h, part).start()
        for step in range(1, hops + 1):
            for h in (1, 0):
                for part in range(2):
                    for d in range(2):
                        if step > length(d, part):
                            continue
                        gather_copy(d, step - 1, h, part).wait_recv()
                        if step < length(d, part):
                            gather_copy(d, step, h, part).start()
                        if h == 0:
                            hand_over(d, step, part).start()
            if step == hops - 3:
                adapter_meet()
            if step == hops - 2:
                adapter_apply()
        for step in range(hops):
            for h in (1, 0):
                for part in range(2):
                    for d in range(2):
                        if step < length(d, part):
                            gather_copy(d, step, h, part).wait_send()
                            if h == 0:
                                hand_over(d, step + 1, part).wait_send()

    @pl.when(core == 0)
    def _():
        block_copy.start()
        adapter_meet()
        adapter_apply()
        for step in range(1, hops + 1):
            for part in range(2):
                for d in range(2):
                    if step <= length(d, part):
                        hand_over(d, step, part).wait_recv()
        block_copy.wait_send()

    for copy in own[:6]:
        copy.wait()
    for copy in shared:
        copy.wait()

    rows = gath[core].reshape(planes * ROWS, width)
    logits = dot_nt(rows, router_ref[...])
    chosen = jnp.sum(jnp.where(iota(logits.shape, 1) == col, logits, 0.0), axis=1, keepdims=True)
    gate_prob = 1.0 / (1.0 + jnp.exp(-chosen))
    for n in range(2):
        gate = dot(rows, w1[n])
        value = gate / (1.0 + jnp.exp(-gate)) * dot(rows, w1[2 + n])
        if n == 1:
            value = value * gate_prob
        hid[:, pl.ds(2 * n * half, 2 * half)] = value.astype(BF)

    @pl.loop(0, width // 256)
    def _(t):
        cols = pl.ds(pl.multiple_of(t * 256, 256), 256)
        product = dot(hid[...], w2[:, cols]).astype(BF)
        pb[core, :, :, cols] = product.reshape(planes, ROWS, 256)

    def give(offset):
        dest = plane(offset)
        return remote(pb.at[0, dest], pb.at[0, dest], psem, (offset,), sibling)

    def reduce_copy(d, step, h, part):
        cols = pl.ds(part * side, side)
        src = first.at[d, h, :, cols] if step == 0 else rb.at[d, step - 1, h, :, cols]
        return remote(src, rb.at[d, step, h, :, cols], qsem, (d, step, h, part), near[d])

    order = [hops]
    for distance in range(hops - 1, 0, -1):
        order += [distance, planes - distance]
    order.append(0)
    y_copy = remote(ystage, yb, ysem, (), sibling)

    @pl.when(core == 0)
    def _():
        for offset in order:
            give(offset).start()
        for offset in order:
            give(offset).wait_send()
        y_copy.wait_recv()

    @pl.when(core == 1)
    def _():
        given = set()
        for step in range(hops + 1):
            for h in (1, 0):
                for part in range(2):
                    cols = pl.ds(part * side, side)
                    for d in range(2):
                        n = length(d, part)
                        if step >= n:
                            continue
                        offset = n - step if d == 0 else planes - n + step
                        if h == 0 and offset not in given:
                            give(offset).wait_recv()
                            given.add(offset)
                        dest = plane(offset)
                        if step == 0:
                            first[d, h, :, cols] = pb[h, dest, :, cols]
                        else:
                            reduce_copy(d, step - 1, h, part).wait_recv()
                            rb[d, step - 1, h, :, cols] = (
                                rb[d, step - 1, h, :, cols].astype(F32)
                                + pb[h, dest, :, cols].astype(F32)
                            ).astype(BF)
                        reduce_copy(d, step, h, part).start()
        give(0).wait_recv()
        for h in (0, 1):
            for part in range(2):
                cols = pl.ds(part * side, side)
                value = pb[h, z, :, cols].astype(F32)
                for d in range(2):
                    last = length(d, part) - 1
                    reduce_copy(d, last, h, part).wait_recv()
                    value = value + rb[d, last, h, :, cols].astype(F32)
                if h == 0:
                    ystage[:, cols] = value.astype(BF)
                else:
                    yb[:, cols] = value.astype(BF)
            if h == 0:
                y_copy.start()
        for step in range(hops):
            for h in (1, 0):
                for part in range(2):
                    for d in range(2):
                        if step < length(d, part):
                            reduce_copy(d, step, h, part).wait_send()
        y_copy.wait_send()

    rs[...] = dot_t(pack_ref[...], stack(yb[...], 0.0)).astype(BF).reshape(rs.shape)
    start_all(over_columns, rs, rr, rsem, columns)
    rr[col] = rs[col]

    wait_all(over_planes, bs, br, bsem, planes)
    swap = remote(br, br2, exsem, (1,), sibling)
    swap.start()
    stored = spread(storage, wide_index)
    my_half = jnp.bitwise_and(wide_lane // PACK, 1) == core
    owner = wide_lane // pairs * 2
    swap.wait()
    total = dot(
        one_hot(wide_piece & my_half & (stored == owner + core)), br[...].reshape(outer, -1)
    )
    total += dot(
        one_hot(wide_piece & my_half & (stored == owner + 1 - core)), br2[...].reshape(outer, -1)
    )
    wait_all(over_columns, rs, rr, rsem, columns)
    from_expert = one_hot(wide_piece & (spread(route_slot, wide_index) == wide_lane // PACK))
    total += dot(from_expert, rr[...].reshape(outer, -1))
    for i in range(tiles):
        cols = pl.ds(i * LANES, LANES)
        value = tok[:, cols] + tile_of(total, i)
        out_ref[:, cols] = value[:sessions].astype(BF)


def body(
    tokens,
    norm_scale_vector,
    router,
    routes,
    session_speaker,
    adapter_slots,
    speaker_down_weight,
    speaker_up_weight,
    routed_gate_weight,
    routed_up_weight,
    routed_down_weight,
    common_gate_weight,
    common_up_weight,
    common_down_weight,
):
    sessions, width = tokens.shape
    planes = lax.axis_size("dp") // 2
    columns = lax.axis_size("expert")
    half = common_gate_weight.shape[1]
    rank = speaker_down_weight.shape[2]
    hops = planes // 2
    vmem = pl.BlockSpec(memory_space=pltpu.VMEM)
    smem = pl.BlockSpec(memory_space=pltpu.SMEM)
    hbm = pl.BlockSpec(memory_space=pl.ANY)
    dma = pltpu.SemaphoreType.DMA
    packed = pltpu.VMEM((columns, 2 * PACK, 3 * LANES), BF)
    over_z = pltpu.VMEM((planes, 2 * PACK, 3 * LANES), BF)
    return pl.pallas_call(
        functools.partial(block_kernel, planes, columns),
        out_shape=jax.ShapeDtypeStruct((sessions, width), BF),
        in_specs=[smem] * 3 + [vmem] * 3 + [hbm] * 8,
        out_specs=vmem,
        scratch_shapes=[
            pltpu.VMEM((ROWS, width), F32),
            pltpu.VMEM((4, width, 2 * half), BF),
            pltpu.VMEM((4 * half, width), BF),
            pltpu.VMEM((rank, width), BF),
            pltpu.VMEM((rank, width), BF),
            packed,
            packed,
            over_z,
            over_z,
            over_z,
            packed,
            packed,
            over_z,
            over_z,
            over_z,
            pltpu.VMEM((PACK * ROWS, columns * 2 * PACK), BF),
            pltpu.VMEM((2, planes, ROWS, width), BF),
            pltpu.VMEM((planes * ROWS, 4 * half), BF),
            pltpu.VMEM((2, planes, ROWS, width), BF),
            pltpu.VMEM((2, 2, ROWS, width), BF),
            pltpu.VMEM((2, hops, 2, ROWS, width), BF),
            pltpu.VMEM((ROWS, width), BF),
            pltpu.VMEM((ROWS, width), BF),
            dma((8,)),
            dma((2, 6)),
            dma((2, columns)),
            dma((2, planes)),
            dma((2, columns)),
            dma((2, planes)),
            dma((2, 2)),
            dma((2,)),
            dma((2, 2, hops, 2, 2)),
            dma((2, 2, hops + 1, 2)),
            dma((2, planes)),
            dma((2, 2, hops, 2, 2)),
            dma((2,)),
        ],
        compiler_params=pltpu.CompilerParams(
            collective_id=1, has_side_effects=True, vmem_limit_bytes=56 * 1024 * 1024
        ),
    )(
        routes,
        session_speaker,
        adapter_slots,
        tokens,
        norm_scale_vector[None],
        router.T,
        common_gate_weight[None],
        routed_gate_weight,
        common_up_weight[None],
        routed_up_weight,
        common_down_weight[None],
        routed_down_weight,
        speaker_down_weight,
        speaker_up_weight,
    )


def solution(mesh):
    in_specs = (
        P(("dp", "expert"), None),
        P(),
        P(),
        P(("dp", "expert")),
        P(("dp", "expert")),
        P("expert", None),
        P("expert", "dp", None, None),
        P("expert", "dp", None, None),
        P("expert", None, "dp"),
        P("expert", None, "dp"),
        P("expert", "dp", None),
        P(None, "dp"),
        P(None, "dp"),
        P("dp", None),
    )
    out_specs = P(("dp", "expert"), None)
    return jax.shard_map(body, mesh=mesh, in_specs=in_specs, out_specs=out_specs, check_vma=False)
```

```python
import functools

import jax
import jax.numpy as jnp
from jax import lax
from jax.experimental import pallas as pl
from jax.experimental.pallas import tpu as pltpu
from jax.sharding import PartitionSpec as P

MESH = pl.DeviceIdType.MESH
BF = jnp.bfloat16
F32 = jnp.float32
I32 = jnp.int32
norm_eps = 1e-05
ROWS = 16
LANES = 128
PACK = 8


def iota(shape, dim):
    return lax.broadcasted_iota(I32, shape, dim)


def one_hot(condition):
    return jnp.where(condition, 1.0, 0.0).astype(BF)


def stack(rows, fill):
    tiles = rows.shape[1] // LANES
    columns = []
    for t in range(-(-tiles // PACK)):
        pieces = []
        for j in range(PACK):
            i = t * PACK + j
            if i < tiles:
                pieces.append(rows[:, i * LANES : (i + 1) * LANES])
            else:
                pieces.append(jnp.full((ROWS, LANES), fill if i == tiles else 0.0, rows.dtype))
        columns.append(jnp.concatenate(pieces, axis=0))
    return jnp.concatenate(columns, axis=1)


def tile_of(stacked, i):
    t, j = i // PACK, i % PACK
    return stacked[j * ROWS : (j + 1) * ROWS, t * LANES : (t + 1) * LANES]


def unstack(stacked, tiles):
    return jnp.concatenate([tile_of(stacked, i) for i in range(tiles)], axis=1)


def dot(a, b):
    return jnp.dot(a, b, preferred_element_type=F32)


def dot_t(a, b):
    return lax.dot_general(a, b, (((0,), (0,)), ((), ())), preferred_element_type=F32)


def dot_nt(a, b):
    return lax.dot_general(a, b, (((1,), (1,)), ((), ())), preferred_element_type=F32)


def block_kernel(
    planes,
    columns,
    routes_ref,
    speaker_ref,
    slots_ref,
    tokens_ref,
    gain_ref,
    router_ref,
    cg_ref,
    rg_ref,
    cu_ref,
    ru_ref,
    cd_ref,
    rd_ref,
    down_ref,
    up_ref,
    out_ref,
    tok,
    w1,
    w2,
    wd,
    wu,
    xs,
    xr,
    ls,
    ls2,
    ls4,
    lr,
    rs,
    rr,
    bs,
    br,
    pack_ref,
    gath,
    hid,
    pb,
    first,
    rb,
    ystage,
    yb,
    own_sem,
    wsem,
    xsem,
    lsem,
    rsem,
    bsem,
    exsem,
    blksem,
    gsem,
    dsem,
    psem,
    qsem,
    ysem,
):
    dp = lax.axis_index("dp")
    col = lax.axis_index("expert")
    z = dp // 2
    core = lax.rem(dp, 2)
    sessions, width = tokens_ref.shape
    tiles = width // LANES
    half = cg_ref.shape[2]
    hops = planes // 2
    side = width // 2
    sibling = (z * 2 + 1 - core, col)

    def plane(offset):
        return lax.rem(z + offset, planes)

    def remote(src, dst, sem, index, device):
        return pltpu.make_async_remote_copy(
            src,
            dst,
            sem.at[(0, *index)],
            sem.at[(1, *index)],
            device_id=device,
            device_id_type=MESH,
        )

    barrier = pltpu.get_barrier_semaphore()

    def greet(device):
        pl.semaphore_signal(barrier, inc=1, device_id=device, device_id_type=MESH)

    near = ((plane(1) * 2 + core, col), (plane(planes - 1) * 2 + core, col))
    greet(sibling)
    for d in range(1, columns):
        greet((dp, lax.rem(col + d, columns)))

    @pl.when(core == 1)
    def _():
        for device in near:
            greet(device)

    @pl.when(core == 0)
    def _():
        for d in range(1, planes):
            greet((plane(d) * 2, col))

    sources = (cg_ref, rg_ref, cu_ref, ru_ref)
    own = []
    for j in range(4):
        own.append(
            pltpu.make_async_copy(sources[j].at[0], w1.at[j, :, pl.ds(0, half)], own_sem.at[j])
        )
    for j, ref in enumerate((cd_ref, rd_ref)):
        own.append(
            pltpu.make_async_copy(ref.at[0], w2.at[pl.ds(2 * j * half, half)], own_sem.at[4 + j])
        )
    for copy in own:
        copy.start()
    adapter = (
        pltpu.make_async_copy(down_ref.at[0, 0], wd.at[0], own_sem.at[6]),
        pltpu.make_async_copy(up_ref.at[0, 0], wu.at[0], own_sem.at[7]),
    )

    @pl.when(core == 0)
    def _():
        for copy in adapter:
            copy.start()

    tok[...] = jnp.zeros_like(tok)
    tok[0:sessions, :] = tokens_ref[...].astype(F32)
    x = tok[...]
    scale = lax.rsqrt(jnp.mean(x * x, axis=-1, keepdims=True) + norm_eps)
    normed = (x * scale * gain_ref[...][None, :]).astype(BF)

    routes = [routes_ref[s] for s in range(sessions)]
    route_slot = []
    for s in range(sessions):
        rank = jnp.int32(0)
        for earlier in range(s):
            rank = rank + jnp.where(routes[earlier] == routes[s], 1, 0)
        route_slot.append(routes[s] * 2 + rank)
    storage = [slots_ref[0, speaker_ref[s]] for s in range(sessions)]

    def spread(values, index):
        held = jnp.full(index.shape, -1, I32)
        for s in range(sessions):
            held = jnp.where(index == s, values[s], held)
        return held

    pairs = 2 * PACK
    outer = columns * pairs
    inner = PACK * ROWS
    row = iota((outer, inner), 0)
    lane = iota((outer, inner), 1)
    lane_session = jnp.bitwise_and(iota((1, inner), 1), ROWS - 1)
    same_piece = jnp.bitwise_and(row, PACK - 1) == lane // ROWS
    stacked = stack(normed, 1.0)
    to_expert = one_hot(same_piece & (row // PACK == spread(route_slot, lane_session)))
    xs[...] = dot(to_expert, stacked).astype(BF).reshape(xs.shape)
    to_adapter = one_hot(same_piece & (row // PACK == spread(storage, lane_session)))
    tail = stacked[: inner // 2, 2 * LANES :]
    tail = jnp.concatenate([tail, tail], axis=0)
    tail = jnp.where(iota(tail.shape, 0) // (inner // 2) == core, tail.astype(F32), 0.0).astype(BF)
    stacked = jnp.concatenate([stacked[:, : 2 * LANES], tail], axis=1)
    ls[...] = dot(to_adapter, stacked).astype(BF).reshape(ls.shape)

    def over_columns(src, dst, sem, d):
        to = lax.rem(col + d, columns)
        return remote(src.at[to], dst.at[col], sem, (d,), (dp, to))

    def over_planes(src, dst, sem, d):
        to = plane(d)
        return remote(src.at[to], dst.at[z], sem, (d,), (to * 2 + core, col))

    def start_all(over, src, dst, sem, count):
        for d in range(1, count):
            over(src, dst, sem, d).start()

    def wait_all(over, src, dst, sem, count):
        for d in range(1, count):
            over(src, dst, sem, d).wait()

    slots_copy = remote(ls, ls2, exsem, (0,), sibling)
    adapter_copies = (
        remote(down_ref.at[0, 0], wd.at[1], wsem, (6,), sibling),
        remote(up_ref.at[0, 0], wu.at[1], wsem, (7,), sibling),
    )

    @pl.when(core == 1)
    def _():
        pl.semaphore_wait(barrier, columns + 2)
        slots_copy.start()

    @pl.when(core == 0)
    def _():
        pl.semaphore_wait(barrier, columns + planes - 1)

    start_all(over_columns, xs, xr, xsem, columns)
    xr[col] = xs[col]

    @pl.when(core == 0)
    def _():
        slots_copy.wait_recv()
        ls4[:, :, 0 : 2 * LANES] = ls[:, :, 0 : 2 * LANES]
        ls4[:, :, 2 * LANES : 4 * LANES] = ls2[:, :, 0 : 2 * LANES]
        ls4[:, :, 4 * LANES :] = ls[:, :, 2 * LANES :] + ls2[:, :, 2 * LANES :]
        start_all(over_planes, ls4, lr, lsem, planes)
        lr[z] = ls4[z]

    shared = []
    for j in range(4):
        shared.append(
            remote(sources[j].at[0], w1.at[j, :, pl.ds(half, half)], wsem, (j,), sibling)
        )
    for j, ref in enumerate((cd_ref, rd_ref)):
        shared.append(
            remote(ref.at[0], w2.at[pl.ds((2 * j + 1) * half, half)], wsem, (4 + j,), sibling)
        )
    for copy in shared:
        copy.start()

    @pl.when(core == 1)
    def _():
        for copy in adapter_copies:
            copy.start()

    wait_all(over_columns, xs, xr, xsem, columns)
    arrived = xr[...].reshape(outer, 3 * LANES)
    flags = jnp.where(
        jnp.bitwise_and(row, PACK - 1) == tiles % PACK, arrived[:, 2 * LANES :], 0.0
    ).astype(BF)
    left = iota((outer, outer), 0) // PACK
    right = iota((outer, outer), 1) // PACK
    before = dot_t(flags, one_hot(left < right))
    taken = dot_t(flags, one_hot(left == right))
    wide_row = iota((inner, outer), 0)
    wide_lane = iota((inner, outer), 1)
    wide_piece = wide_row // ROWS == jnp.bitwise_and(wide_lane, PACK - 1)
    wide_index = jnp.bitwise_and(wide_row, ROWS - 1)
    pack_ref[...] = one_hot(
        wide_piece & (taken > 0.5) & (jnp.abs(before - wide_index.astype(F32)) < 0.5)
    )
    mine = pl.ds(pl.multiple_of(core * ROWS, ROWS), ROWS)
    gath[z, mine, :] = unstack(dot(pack_ref[...], arrived).astype(BF), tiles)

    def pick(half_index):
        return one_hot(
            wide_piece
            & (wide_index == wide_lane // pairs)
            & (jnp.bitwise_and(wide_lane // PACK, 1) == half_index)
        )

    def adapter_apply():
        wait_all(over_planes, ls4, lr, lsem, planes)
        for copy in adapter:
            copy.wait()
        for copy in adapter_copies:
            copy.wait_recv()
        back = jnp.zeros((outer, 5 * LANES), F32)
        for r in range(2):
            chosen = pick(r)
            got = dot(chosen, lr[...].reshape(outer, 5 * LANES)).astype(BF)
            parts = []
            for source in range(2):
                pieces = []
                for i in range(tiles):
                    t, j = i // PACK, i % PACK
                    if t == 2:
                        t, j = 4, j + 4 * source
                    else:
                        t = t + 2 * source
                    pieces.append(got[j * ROWS : (j + 1) * ROWS, t * LANES : (t + 1) * LANES])
                parts.append(jnp.concatenate(pieces, axis=1))
            low = dot_nt(jnp.concatenate(parts, axis=0), wd[r]).astype(BF)
            delta = dot(low, wu[r]).astype(BF)
            first_stack, second_stack = stack(delta[:ROWS], 0.0), stack(delta[ROWS:], 0.0)
            both = jnp.concatenate(
                [first_stack[: inner // 2, 2 * LANES :], second_stack[: inner // 2, 2 * LANES :]],
                axis=0,
            )
            back += dot_t(
                chosen,
                jnp.concatenate(
                    [first_stack[:, : 2 * LANES], second_stack[:, : 2 * LANES], both], axis=1
                ),
            )
        bs[...] = back.astype(BF).reshape(bs.shape)
        start_all(over_planes, bs, br, bsem, planes)
        br[z] = bs[z]

    def length(d, part):
        return hops if part == d else hops - 1

    def from_plane(d, step):
        return plane(planes - step if d == 0 else step)

    def gather_copy(d, step, h, part):
        piece = gath.at[from_plane(d, step), pl.ds(h * ROWS, ROWS), pl.ds(part * side, side)]
        return remote(piece, piece, gsem, (d, step, h, part), near[d])

    def hand_over(d, step):
        piece = gath.at[from_plane(d, step)]
        return remote(piece, piece, dsem, (d, step), sibling)

    block_copy = remote(gath.at[z, mine, :], gath.at[z, mine, :], blksem, (), sibling)

    reach = hops - 2
    middle = reach // 2
    inner_planes = [0]
    outer_planes = []
    for distance in range(1, reach + 1):
        both = [distance, planes - distance]
        if distance <= middle:
            inner_planes += both
        else:
            outer_planes = both + outer_planes
    given_planes = outer_planes + inner_planes[:0:-1] + [0]

    def weights_here():
        for copy in own:
            copy.wait()
        for copy in shared:
            copy.wait()

    def apply_experts(offsets):
        rows = jnp.concatenate([gath[plane(o)] for o in offsets], axis=0)
        logits = dot_nt(rows, router_ref[...])
        chosen = jnp.where(iota(logits.shape, 1) == col, logits, 0.0)
        gate_prob = 1.0 / (1.0 + jnp.exp(-jnp.sum(chosen, axis=1, keepdims=True)))
        held = pl.ds(0, len(offsets) * 2 * ROWS)
        for n in range(2):
            gate = dot(rows, w1[n])
            value = gate / (1.0 + jnp.exp(-gate)) * dot(rows, w1[2 + n])
            if n == 1:
                value = value * gate_prob
            hid[held, pl.ds(2 * n * half, 2 * half)] = value.astype(BF)

        @pl.loop(0, width // 256)
        def _(t):
            cols = pl.ds(pl.multiple_of(t * 256, 256), 256)
            product = dot(hid[held, :], w2[:, cols]).astype(BF)
            for i, o in enumerate(offsets):
                pb[plane(o), :, cols] = product[i * 2 * ROWS : (i + 1) * 2 * ROWS]

    def give(offset):
        dest = plane(offset)
        return remote(pb.at[dest], pb.at[dest], psem, (offset,), sibling)

    def reduce_copy(d, step, h, part):
        place = (pl.ds(h * ROWS, ROWS), pl.ds(part * side, side))
        src = first.at[(d, *place)] if step == 0 else rb.at[(d, step - 1, *place)]
        return remote(src, rb.at[(d, step, *place)], qsem, (d, step, h, part), near[d])

    def reduce_step(step, chain, given):
        for h in (1, 0):
            for d in range(2):
                part = d if chain == hops else 1 - d
                place = (pl.ds(h * ROWS, ROWS), pl.ds(part * side, side))
                offset = chain - step if d == 0 else planes - chain + step
                if offset in given_planes and offset not in given:
                    give(offset).wait_recv()
                    given.add(offset)
                dest = plane(offset)
                if step == 0:
                    first[(d, *place)] = pb[(dest, *place)]
                else:
                    reduce_copy(d, step - 1, h, part).wait_recv()
                    rb[(d, step - 1, *place)] = (
                        rb[(d, step - 1, *place)].astype(F32) + pb[(dest, *place)].astype(F32)
                    ).astype(BF)
                reduce_copy(d, step, h, part).start()

    @pl.when(core == 1)
    def _():
        block_copy.start()
        for h in (1, 0):
            if h == 0:
                block_copy.wait_recv()
            for part in range(2):
                for d in range(2):
                    gather_copy(d, 0, h, part).start()
        for step in range(1, hops + 1):
            if step == hops:
                weights_here()
                apply_experts([hops - 1, planes - hops + 1])
                reduce_step(0, hops - 1, set())
            for h in (1, 0):
                for part in range(2):
                    for d in range(2):
                        if step > length(d, part):
                            continue
                        gather_copy(d, step - 1, h, part).wait_recv()
                        if step < length(d, part):
                            gather_copy(d, step, h, part).start()
            if step <= reach:
                for d in range(2):
                    hand_over(d, step).start()
        apply_experts([hops])
        reduce_step(0, hops, set())

    @pl.when(core == 0)
    def _():
        block_copy.start()
        weights_here()
        block_copy.wait_recv()
        for step in range(1, reach + 1):
            for d in range(2):
                hand_over(d, step).wait_recv()
            if step == middle:
                apply_experts(inner_planes)
        apply_experts(outer_planes)
        for offset in given_planes:
            give(offset).start()
        adapter_apply()

    y_copy = remote(ystage, yb, ysem, (), sibling)
    delta_copy = remote(br, br, exsem, (1,), sibling)

    @pl.when(core == 0)
    def _():
        wait_all(over_planes, bs, br, bsem, planes)
        delta_copy.start()
        block_copy.wait_send()
        for offset in given_planes:
            give(offset).wait_send()
        delta_copy.wait_send()
        y_copy.wait_recv()

    @pl.when(core == 1)
    def _():
        given = set()
        for step in range(1, hops):
            for chain in (hops - 1, hops):
                if step < chain:
                    reduce_step(step, chain, given)
        give(0).wait_recv()
        for h in (0, 1):
            for part in range(2):
                cols = pl.ds(part * side, side)
                rows = pl.ds(h * ROWS, ROWS)
                value = pb[z, rows, cols].astype(F32)
                for d in range(2):
                    last = length(d, part) - 1
                    reduce_copy(d, last, h, part).wait_recv()
                    value = value + rb[d, last, rows, cols].astype(F32)
                if h == 0:
                    ystage[:, cols] = value.astype(BF)
                else:
                    yb[:, cols] = value.astype(BF)
            if h == 0:
                y_copy.start()

    rs[...] = dot_t(pack_ref[...], stack(yb[...], 0.0)).astype(BF).reshape(rs.shape)
    start_all(over_columns, rs, rr, rsem, columns)
    rr[col] = rs[col]

    @pl.when(core == 1)
    def _():
        slots_copy.wait_send()
        for copy in adapter_copies:
            copy.wait_send()
        for step in range(hops):
            for h in (1, 0):
                for part in range(2):
                    for d in range(2):
                        if step < length(d, part):
                            gather_copy(d, step, h, part).wait_send()
                            reduce_copy(d, step, h, part).wait_send()
        for step in range(1, reach + 1):
            for d in range(2):
                hand_over(d, step).wait_send()
        block_copy.wait_send()
        y_copy.wait_send()
        delta_copy.wait_recv()

    stored = spread(storage, wide_index) == wide_lane // PACK
    body_part = br[:, :, pl.ds(pl.multiple_of(core * 2 * LANES, 2 * LANES), 2 * LANES)]
    tail_part = br[:, :, 4 * LANES :].reshape(outer, LANES)
    tail_piece = wide_row // ROWS + 4 * core == jnp.bitwise_and(wide_lane, PACK - 1)
    total = jnp.concatenate(
        [
            dot(one_hot(wide_piece & stored), body_part.reshape(outer, 2 * LANES)),
            dot(one_hot(tail_piece & stored), tail_part),
        ],
        axis=1,
    )
    wait_all(over_columns, rs, rr, rsem, columns)
    from_expert = one_hot(wide_piece & (spread(route_slot, wide_index) == wide_lane // PACK))
    total += dot(from_expert, rr[...].reshape(outer, -1))
    for i in range(tiles):
        cols = pl.ds(i * LANES, LANES)
        value = tok[:, cols] + tile_of(total, i)
        out_ref[:, cols] = value[:sessions].astype(BF)


def body(
    tokens,
    norm_scale_vector,
    router,
    routes,
    session_speaker,
    adapter_slots,
    speaker_down_weight,
    speaker_up_weight,
    routed_gate_weight,
    routed_up_weight,
    routed_down_weight,
    common_gate_weight,
    common_up_weight,
    common_down_weight,
):
    sessions, width = tokens.shape
    planes = lax.axis_size("dp") // 2
    columns = lax.axis_size("expert")
    half = common_gate_weight.shape[1]
    rank = speaker_down_weight.shape[2]
    hops = planes // 2
    vmem = pl.BlockSpec(memory_space=pltpu.VMEM)
    smem = pl.BlockSpec(memory_space=pltpu.SMEM)
    hbm = pl.BlockSpec(memory_space=pl.ANY)
    dma = pltpu.SemaphoreType.DMA
    packed = pltpu.VMEM((columns, 2 * PACK, 3 * LANES), BF)
    over_z = pltpu.VMEM((planes, 2 * PACK, 3 * LANES), BF)
    wide_z = pltpu.VMEM((planes, 2 * PACK, 5 * LANES), BF)
    return pl.pallas_call(
        functools.partial(block_kernel, planes, columns),
        out_shape=jax.ShapeDtypeStruct((sessions, width), BF),
        in_specs=[smem] * 3 + [vmem] * 3 + [hbm] * 8,
        out_specs=vmem,
        scratch_shapes=[
            pltpu.VMEM((ROWS, width), F32),
            pltpu.VMEM((4, width, 2 * half), BF),
            pltpu.VMEM((4 * half, width), BF),
            pltpu.VMEM((2, rank, width), BF),
            pltpu.VMEM((2, rank, width), BF),
            packed,
            packed,
            over_z,
            over_z,
            wide_z,
            wide_z,
            packed,
            packed,
            wide_z,
            wide_z,
            pltpu.VMEM((PACK * ROWS, columns * 2 * PACK), BF),
            pltpu.VMEM((planes, 2 * ROWS, width), BF),
            pltpu.VMEM((planes * ROWS, 4 * half), BF),
            pltpu.VMEM((planes, 2 * ROWS, width), BF),
            pltpu.VMEM((2, 2 * ROWS, width), BF),
            pltpu.VMEM((2, hops, 2 * ROWS, width), BF),
            pltpu.VMEM((ROWS, width), BF),
            pltpu.VMEM((ROWS, width), BF),
            dma((8,)),
            dma((2, 8)),
            dma((2, columns)),
            dma((2, planes)),
            dma((2, columns)),
            dma((2, planes)),
            dma((2, 2)),
            dma((2,)),
            dma((2, 2, hops, 2, 2)),
            dma((2, 2, hops)),
            dma((2, planes)),
            dma((2, 2, hops, 2, 2)),
            dma((2,)),
        ],
        compiler_params=pltpu.CompilerParams(
            collective_id=1, has_side_effects=True, vmem_limit_bytes=56 * 1024 * 1024
        ),
    )(
        routes,
        session_speaker,
        adapter_slots,
        tokens,
        norm_scale_vector,
        router.T,
        common_gate_weight[None],
        routed_gate_weight,
        common_up_weight[None],
        routed_up_weight,
        common_down_weight[None],
        routed_down_weight,
        speaker_down_weight,
        speaker_up_weight,
    )


def solution(mesh):
    in_specs = (
        P(("dp", "expert"), None),
        P(),
        P(),
        P(("dp", "expert")),
        P(("dp", "expert")),
        P("expert", None),
        P("expert", "dp", None, None),
        P("expert", "dp", None, None),
        P("expert", None, "dp"),
        P("expert", None, "dp"),
        P("expert", "dp", None),
        P(None, "dp"),
        P(None, "dp"),
        P("dp", None),
    )
    out_specs = P(("dp", "expert"), None)
    return jax.shard_map(body, mesh=mesh, in_specs=in_specs, out_specs=out_specs, check_vma=False)
```

```python
import functools

import jax
import jax.numpy as jnp
from jax import lax
from jax.experimental import pallas as pl
from jax.experimental.pallas import tpu as pltpu
from jax.sharding import PartitionSpec as P

MESH = pl.DeviceIdType.MESH
BF = jnp.bfloat16
F32 = jnp.float32
I32 = jnp.int32
norm_eps = 1e-05
ROWS = 16
REAL = 13
LANES = 128
PACK = 8


def iota(shape, dim):
    return lax.broadcasted_iota(I32, shape, dim)


def one_hot(condition):
    return jnp.where(condition, 1.0, 0.0).astype(BF)


def stack(rows, fill):
    tiles = rows.shape[1] // LANES
    columns = []
    for t in range(-(-tiles // PACK)):
        pieces = []
        for j in range(PACK):
            i = t * PACK + j
            if i < tiles:
                pieces.append(rows[:, i * LANES : (i + 1) * LANES])
            else:
                pieces.append(jnp.full((ROWS, LANES), fill if i == tiles else 0.0, rows.dtype))
        columns.append(jnp.concatenate(pieces, axis=0))
    return jnp.concatenate(columns, axis=1)


def tile_of(stacked, i):
    t, j = i // PACK, i % PACK
    return stacked[j * ROWS : (j + 1) * ROWS, t * LANES : (t + 1) * LANES]


def unstack(stacked, tiles):
    return jnp.concatenate([tile_of(stacked, i) for i in range(tiles)], axis=1)


def tight_tiles(tiles):
    return next(n for n in range(tiles) if (tiles - n) <= ROWS - REAL and REAL <= n)


def moving(n, axis):
    shape = (n * ROWS, (ROWS - REAL) * ROWS)
    a, b = iota(shape[::-1], 1) if axis else iota(shape, 0), iota(shape[::-1], 0) if axis else iota(shape, 1)
    return one_hot((a // ROWS == jnp.bitwise_and(b, ROWS - 1)) & (jnp.bitwise_and(a, ROWS - 1) == REAL + b // ROWS))


def overflow_of(block):
    below = jnp.concatenate([block[:, i * LANES : (i + 1) * LANES] for i in range(REAL)], axis=0)
    return dot(moving(REAL, 1), below).astype(BF)


def tighten(overflow, n):
    placed = dot(moving(n, 0), overflow)
    return jnp.concatenate([placed[i * ROWS : (i + 1) * ROWS] for i in range(n)], axis=1)


def dot(a, b):
    return jnp.dot(a, b, preferred_element_type=F32)


def dot_t(a, b):
    return lax.dot_general(a, b, (((0,), (0,)), ((), ())), preferred_element_type=F32)


def dot_nt(a, b):
    return lax.dot_general(a, b, (((1,), (1,)), ((), ())), preferred_element_type=F32)


def block_kernel(
    planes,
    columns,
    routes_in,
    speaker_in,
    slots_in,
    tokens_ref,
    gain_in,
    router_in,
    cg_ref,
    rg_ref,
    cu_ref,
    ru_ref,
    cd_ref,
    rd_ref,
    down_ref,
    up_ref,
    out_ref,
    routes_ref,
    speaker_ref,
    slots_ref,
    gain_ref,
    router_ref,
    in_sem,
    tok,
    w1,
    w2,
    wd,
    wu,
    xs,
    xr,
    ls,
    ls2,
    ls4,
    lr,
    rs,
    rr,
    bs,
    br,
    pack_ref,
    gath,
    hid,
    pb,
    first,
    rb,
    yb,
    own_sem,
    wsem,
    sent,
    got,
    exsem,
    ring_got,
    over_got,
    give_got,
):
    dp = lax.axis_index("dp")
    col = lax.axis_index("expert")
    z = dp // 2
    core = lax.rem(dp, 2)
    sessions, width = tokens_ref.shape
    tiles = width // LANES
    half = cg_ref.shape[2]
    hops = planes // 2
    tight = tight_tiles(tiles)
    left_out = tiles - tight
    cut = (tight + 1) // 2 * LANES
    sides = (pl.ds(0, cut), pl.ds(cut, tight * LANES - cut))
    sibling = (z * 2 + 1 - core, col)

    def plane(offset):
        return lax.rem(z + offset, planes)

    def remote(src, dst, send_sem, recv_sem, device):
        return pltpu.make_async_remote_copy(
            src, dst, send_sem, recv_sem, device_id=device, device_id_type=MESH
        )

    def group(view, index):
        return remote(view, view, sent.at[index], got.at[index], sibling)

    DISPATCH, RETURN, TO_ADAPTER, FROM_ADAPTER, GATHER, REDUCE, OVER, GIVE = 0, 2, 4, 5, 6, 7, 8, 9

    barrier = pltpu.get_barrier_semaphore()

    def greet(device):
        pl.semaphore_signal(barrier, inc=1, device_id=device, device_id_type=MESH)

    ring = 1
    while ring * ring < columns:
        ring += 1
    assert ring * ring == columns
    far_first = sorted(
        ((i, j) for i in range(ring) for j in range(ring)),
        key=lambda at: -sum(min(a, ring - a) for a in at),
    )

    def column(d):
        i, j = far_first[d]
        return lax.rem(col // ring + i, ring) * ring + lax.rem(lax.rem(col, ring) + j, ring)

    home = columns - 1
    near = ((plane(1) * 2 + core, col), (plane(planes - 1) * 2 + core, col))

    @pl.when(core == 1)
    def _():
        for device in near:
            greet(device)
        for d in range(home):
            greet((z * 2, column(d)))
            greet((z * 2 + 1, column(d)))
        greet(sibling)

    @pl.when(core == 0)
    def _():
        for d in range(1, planes):
            greet((plane(d) * 2, col))
        for d in range(columns):
            greet((z * 2 + 1, column(d)))

    fetched = (
        (routes_in, routes_ref),
        (speaker_in, speaker_ref),
        (slots_in, slots_ref),
        (gain_in, gain_ref),
        (router_in, router_ref),
    )
    fetches = [
        pltpu.make_async_copy(src, dst, in_sem.at[i]) for i, (src, dst) in enumerate(fetched)
    ]
    for copy in fetches:
        copy.start()
    for copy in fetches:
        copy.wait()

    tok[...] = jnp.zeros_like(tok)
    tok[0:sessions, :] = tokens_ref[...].astype(F32)
    x = tok[...]
    scale = lax.rsqrt(jnp.mean(x * x, axis=-1, keepdims=True) + norm_eps)
    normed = (x * scale * gain_ref[...][None, :]).astype(BF)

    routes = [routes_ref[s] for s in range(sessions)]
    route_slot = []
    for s in range(sessions):
        rank = jnp.int32(0)
        for earlier in range(s):
            rank = rank + jnp.where(routes[earlier] == routes[s], 1, 0)
        route_slot.append(routes[s] * 2 + rank)
    storage = [slots_ref[0, speaker_ref[s]] for s in range(sessions)]

    def spread(values, index):
        held = jnp.full(index.shape, -1, I32)
        for s in range(sessions):
            held = jnp.where(index == s, values[s], held)
        return held

    pairs = 2 * PACK
    outer = columns * pairs
    inner = PACK * ROWS
    row = iota((outer, inner), 0)
    lane = iota((outer, inner), 1)
    lane_session = jnp.bitwise_and(iota((1, inner), 1), ROWS - 1)
    same_piece = jnp.bitwise_and(row, PACK - 1) == lane // ROWS
    stacked = stack(normed, 1.0)
    to_expert = one_hot(same_piece & (row // PACK == spread(route_slot, lane_session)))
    xs[...] = dot(to_expert, stacked).astype(BF).reshape(xs.shape)
    def dispatch(d, source):
        return remote(
            xs.at[column(d)],
            xr.at[source, col],
            sent.at[DISPATCH + source],
            got.at[DISPATCH + source],
            (z * 2 + 1, column(d)),
        )

    def bring_back(d, h):
        return remote(
            rs.at[h, column(d)],
            rr.at[col],
            sent.at[RETURN + h],
            got.at[RETURN],
            (z * 2 + h, column(d)),
        )

    def over_planes(src, dst, index):
        for d in range(1, planes):
            to = plane(d)
            remote(src.at[to], dst.at[z], sent.at[index], got.at[index], (to * 2, col)).start()

    slots_copy = remote(ls, ls2, exsem.at[0, 0], exsem.at[1, 0], sibling)
    adapter_copies = (
        remote(down_ref.at[0, 0], wd.at[1], wsem.at[0, 6], wsem.at[1, 6], sibling),
        remote(up_ref.at[0, 0], wu.at[1], wsem.at[0, 7], wsem.at[1, 7], sibling),
    )

    @pl.when(core == 1)
    def _():
        pl.semaphore_wait(barrier, 2 * columns + 1)
        for d in range(home):
            dispatch(d, 1).start()
        xr[1, col] = xs[col]

    @pl.when(core == 0)
    def _():
        pl.semaphore_wait(barrier, columns + planes - 1)
        for d in range(columns):
            dispatch(d, 0).start()

    to_adapter = one_hot(same_piece & (row // PACK == spread(storage, lane_session)))
    tail = stacked[: inner // 2, 2 * LANES :]
    tail = jnp.concatenate([tail, tail], axis=0)
    tail = jnp.where(iota(tail.shape, 0) // (inner // 2) == core, tail.astype(F32), 0.0).astype(BF)
    stacked = jnp.concatenate([stacked[:, : 2 * LANES], tail], axis=1)
    ls[...] = dot(to_adapter, stacked).astype(BF).reshape(ls.shape)

    @pl.when(core == 1)
    def _():
        slots_copy.start()

    sources = (cg_ref, rg_ref, cu_ref, ru_ref)
    own = []
    for j in range(4):
        own.append(
            pltpu.make_async_copy(sources[j].at[0], w1.at[j, :, pl.ds(0, half)], own_sem.at[j])
        )
    for j, ref in enumerate((cd_ref, rd_ref)):
        own.append(
            pltpu.make_async_copy(ref.at[0], w2.at[pl.ds(2 * j * half, half)], own_sem.at[4 + j])
        )
    for copy in own:
        copy.start()
    adapter = (
        pltpu.make_async_copy(down_ref.at[0, 0], wd.at[0], own_sem.at[6]),
        pltpu.make_async_copy(up_ref.at[0, 0], wu.at[0], own_sem.at[7]),
    )

    @pl.when(core == 0)
    def _():
        for copy in adapter:
            copy.start()

    @pl.when(core == 0)
    def _():
        slots_copy.wait_recv()
        ls4[:, :, 0 : 2 * LANES] = ls[:, :, 0 : 2 * LANES]
        ls4[:, :, 2 * LANES : 4 * LANES] = ls2[:, :, 0 : 2 * LANES]
        ls4[:, :, 4 * LANES :] = ls[:, :, 2 * LANES :] + ls2[:, :, 2 * LANES :]
        over_planes(ls4, lr, TO_ADAPTER)
        lr[z] = ls4[z]

    shared = []
    for j in range(4):
        shared.append(
            remote(
                sources[j].at[0],
                w1.at[j, :, pl.ds(half, half)],
                wsem.at[0, j],
                wsem.at[1, j],
                sibling,
            )
        )
    for j, ref in enumerate((cd_ref, rd_ref)):
        shared.append(
            remote(
                ref.at[0],
                w2.at[pl.ds((2 * j + 1) * half, half)],
                wsem.at[0, 4 + j],
                wsem.at[1, 4 + j],
                sibling,
            )
        )
    for copy in shared:
        copy.start()

    @pl.when(core == 1)
    def _():
        for copy in adapter_copies:
            copy.start()

    wide_row = iota((inner, outer), 0)
    wide_lane = iota((inner, outer), 1)
    wide_piece = wide_row // ROWS == jnp.bitwise_and(wide_lane, PACK - 1)
    wide_index = jnp.bitwise_and(wide_row, ROWS - 1)

    def close_up(h):
        arrived = xr[h].reshape(outer, 3 * LANES)
        flags = jnp.where(
            jnp.bitwise_and(row, PACK - 1) == tiles % PACK, arrived[:, 2 * LANES :], 0.0
        ).astype(BF)
        left = iota((outer, outer), 0) // PACK
        right = iota((outer, outer), 1) // PACK
        before = dot_t(flags, one_hot(left < right))
        taken = dot_t(flags, one_hot(left == right))
        pack_ref[h] = one_hot(
            wide_piece & (taken > 0.5) & (jnp.abs(before - wide_index.astype(F32)) < 0.5)
        )
        placed = dot(pack_ref[h], arrived)
        over = jnp.concatenate([tile_of(placed, tight + i) for i in range(left_out)], axis=0)
        gath[z, pl.ds(h * ROWS, ROWS), :] = (
            unstack(placed, tight) + tighten(over.astype(BF), tight)
        ).astype(BF)

    def pick(half_index):
        return one_hot(
            wide_piece
            & (wide_index == wide_lane // pairs)
            & (jnp.bitwise_and(wide_lane // PACK, 1) == half_index)
        )

    def adapter_apply():
        group(lr.at[pl.ds(0, planes - 1)], TO_ADAPTER).wait()
        for copy in adapter:
            copy.wait()
        for copy in adapter_copies:
            copy.wait_recv()
        back = jnp.zeros((outer, 5 * LANES), F32)
        for r in range(2):
            chosen = pick(r)
            got = dot(chosen, lr[...].reshape(outer, 5 * LANES)).astype(BF)
            parts = []
            for source in range(2):
                pieces = []
                for i in range(tiles):
                    t, j = i // PACK, i % PACK
                    if t == 2:
                        t, j = 4, j + 4 * source
                    else:
                        t = t + 2 * source
                    pieces.append(got[j * ROWS : (j + 1) * ROWS, t * LANES : (t + 1) * LANES])
                parts.append(jnp.concatenate(pieces, axis=1))
            low = dot_nt(jnp.concatenate(parts, axis=0), wd[r]).astype(BF)
            delta = dot(low, wu[r]).astype(BF)
            first_stack, second_stack = stack(delta[:ROWS], 0.0), stack(delta[ROWS:], 0.0)
            both = jnp.concatenate(
                [first_stack[: inner // 2, 2 * LANES :], second_stack[: inner // 2, 2 * LANES :]],
                axis=0,
            )
            back += dot_t(
                chosen,
                jnp.concatenate(
                    [first_stack[:, : 2 * LANES], second_stack[:, : 2 * LANES], both], axis=1
                ),
            )
        bs[...] = back.astype(BF).reshape(bs.shape)
        over_planes(bs, br, FROM_ADAPTER)
        br[z] = bs[z]

    def length(d, part):
        return hops if part == d else hops - 1

    def from_plane(d, step):
        return plane(planes - step if d == 0 else step)

    def gather_copy(d, step, h, part):
        piece = gath.at[from_plane(d, step), pl.ds(h * ROWS, ROWS), sides[part]]
        return remote(piece, piece, sent.at[GATHER], ring_got.at[d, step, h, part], near[d])

    def hand_over(d, step):
        piece = gath.at[from_plane(d, step)]
        return remote(piece, piece, sent.at[OVER], over_got.at[d, step], sibling)

    reach = hops - 2
    middle = reach // 2
    inner_planes = [0]
    outer_planes = []
    for distance in range(1, reach + 1):
        both = [distance, planes - distance]
        if distance <= middle:
            inner_planes += both
        else:
            outer_planes = both + outer_planes
    given_planes = outer_planes + inner_planes[:0:-1] + [0]

    def weights_here():
        for copy in own:
            copy.wait()
        for copy in shared:
            copy.wait()

    def apply_experts(offsets):
        blocks = []
        for o in offsets:
            for h in range(2):
                block = gath[plane(o), pl.ds(h * ROWS, ROWS), :]
                over = overflow_of(block)
                blocks.append(
                    jnp.concatenate(
                        [block] + [over[i * ROWS : (i + 1) * ROWS] for i in range(left_out)], axis=1
                    )
                )
        rows = jnp.concatenate(blocks, axis=0)
        logits = dot_nt(rows, router_ref[...])
        chosen = jnp.where(iota(logits.shape, 1) == col, logits, 0.0)
        gate_prob = 1.0 / (1.0 + jnp.exp(-jnp.sum(chosen, axis=1, keepdims=True)))
        held = pl.ds(0, len(offsets) * 2 * ROWS)
        holds = jnp.bitwise_and(iota((len(offsets) * 2 * ROWS, 1), 0), ROWS - 1) < REAL
        for n in range(2):
            gate = dot(rows, w1[n])
            value = gate / (1.0 + jnp.exp(-gate)) * dot(rows, w1[2 + n])
            if n == 1:
                value = value * gate_prob
            value = jnp.where(holds, value, 0.0)
            hid[held, pl.ds(2 * n * half, 2 * half)] = value.astype(BF)

        over = dot(hid[held, :], w2[:, tight * LANES :]).astype(BF)
        for i, o in enumerate(offsets):
            for h in range(2):
                k = (i * 2 + h) * ROWS
                pieces = [
                    over[k : k + ROWS, j * LANES : (j + 1) * LANES] for j in range(left_out)
                ]
                pb[plane(o), pl.ds(h * ROWS, ROWS), :] = tighten(
                    jnp.concatenate(pieces, axis=0), tight
                ).astype(BF)

        def add_columns(cols):
            product = dot(hid[held, :], w2[:, cols])
            for i, o in enumerate(offsets):
                k = i * 2 * ROWS
                pb[plane(o), :, cols] = (
                    product[k : k + 2 * ROWS] + pb[plane(o), :, cols].astype(F32)
                ).astype(BF)

        @pl.loop(0, tight // 2)
        def _(t):
            add_columns(pl.ds(pl.multiple_of(t * 2 * LANES, 2 * LANES), 2 * LANES))

        if tight % 2:
            add_columns(pl.ds((tight - 1) * LANES, LANES))

    def give(offset):
        dest = plane(offset)
        return remote(pb.at[dest], pb.at[dest], sent.at[GIVE], give_got.at[offset], sibling)

    def reduce_copy(d, step, h, part):
        place = (pl.ds(h * ROWS, ROWS), sides[part])
        src = first.at[(d, *place)] if step == 0 else rb.at[(d, step - 1, *place)]
        return remote(
            src,
            rb.at[(d, step, *place)],
            sent.at[REDUCE],
            ring_got.at[d, step, h, part],
            near[d],
        )

    def reduce_step(step, chain, given):
        for h in (0, 1):
            for d in range(2):
                part = d if chain == hops else 1 - d
                place = (pl.ds(h * ROWS, ROWS), sides[part])
                offset = chain - step if d == 0 else planes - chain + step
                if offset in given_planes and offset not in given:
                    give(offset).wait_recv()
                    given.add(offset)
                dest = plane(offset)
                if step == 0:
                    first[(d, *place)] = pb[(dest, *place)]
                else:
                    reduce_copy(d, step - 1, h, part).wait_recv()
                    rb[(d, step - 1, *place)] = (
                        rb[(d, step - 1, *place)].astype(F32) + pb[(dest, *place)].astype(F32)
                    ).astype(BF)
                reduce_copy(d, step, h, part).start()

    @pl.when(core == 1)
    def _():
        for h in (1, 0):
            group(xr.at[h, pl.ds(0, columns - h)], DISPATCH + h).wait_recv()
            close_up(h)
            for part in range(2):
                for d in range(2):
                    gather_copy(d, 0, h, part).start()
        hand_over(0, 0).start()
        for step in range(1, hops + 1):
            if step == hops:
                weights_here()
                apply_experts([hops - 1, planes - hops + 1])
                reduce_step(0, hops - 1, set())
            for h in (1, 0):
                for part in range(2):
                    for d in range(2):
                        if step > length(d, part):
                            continue
                        gather_copy(d, step - 1, h, part).wait_recv()
                        if step < length(d, part):
                            gather_copy(d, step, h, part).start()
            if step <= reach:
                for d in range(2):
                    hand_over(d, step).start()
        apply_experts([hops])
        reduce_step(0, hops, set())

    @pl.when(core == 0)
    def _():
        weights_here()
        hand_over(0, 0).wait_recv()
        for step in range(1, reach + 1):
            for d in range(2):
                hand_over(d, step).wait_recv()
            if step == middle:
                apply_experts(inner_planes)
                adapter_apply()
        apply_experts(outer_planes)
        for offset in given_planes:
            give(offset).start()

    delta_copy = remote(br, br, exsem.at[0, 1], exsem.at[1, 1], sibling)

    @pl.when(core == 0)
    def _():
        group(br.at[pl.ds(0, planes - 1)], FROM_ADAPTER).wait()
        delta_copy.start()
        group(pb.at[pl.ds(0, len(given_planes))], GIVE).wait_send()
        delta_copy.wait_send()

    @pl.when(core == 1)
    def _():
        given = set()
        for step in range(1, hops):
            for chain in (hops - 1, hops):
                if step < chain:
                    reduce_step(step, chain, given)
        give(0).wait_recv()
        for h in (0, 1):
            for part in range(2):
                cols = sides[part]
                rows = pl.ds(h * ROWS, ROWS)
                value = pb[z, rows, cols].astype(F32)
                for d in range(2):
                    last = length(d, part) - 1
                    reduce_copy(d, last, h, part).wait_recv()
                    value = value + rb[d, last, rows, cols].astype(F32)
                yb[h, :, cols] = value.astype(BF)
            result = yb[h]
            pieces = [result[:, i * LANES : (i + 1) * LANES] for i in range(tight)]
            over = overflow_of(result)
            pieces += [over[i * ROWS : (i + 1) * ROWS] for i in range(left_out)]
            result = stack(jnp.concatenate(pieces, axis=1), 0.0)
            rs[h] = dot_t(pack_ref[h], result).astype(BF).reshape(rs.shape[1:])
            for d in range(home):
                bring_back(d, h).start()
            if h == 0:
                bring_back(home, h).start()
            else:
                rr[col] = rs[h, col]

    @pl.when(core == 1)
    def _():
        slots_copy.wait_send()
        for copy in adapter_copies:
            copy.wait_send()
        group(gath.at[pl.ds(0, planes - 1)], GATHER).wait_send()
        group(gath.at[pl.ds(0, planes - 1)], REDUCE).wait_send()
        group(gath.at[pl.ds(0, 2 * reach + 1)], OVER).wait_send()
        group(xs.at[pl.ds(0, columns - 1)], DISPATCH + 1).wait_send()
        delta_copy.wait_recv()

    @pl.when(core == 0)
    def _():
        group(xs, DISPATCH).wait_send()

    stored = spread(storage, wide_index) == wide_lane // PACK
    body_part = br[:, :, pl.ds(pl.multiple_of(core * 2 * LANES, 2 * LANES), 2 * LANES)]
    tail_part = br[:, :, 4 * LANES :].reshape(outer, LANES)
    tail_piece = wide_row // ROWS + 4 * core == jnp.bitwise_and(wide_lane, PACK - 1)
    total = jnp.concatenate(
        [
            dot(one_hot(wide_piece & stored), body_part.reshape(outer, 2 * LANES)),
            dot(one_hot(tail_piece & stored), tail_part),
        ],
        axis=1,
    )
    @pl.when(core == 1)
    def _():
        group(rr.at[pl.ds(0, columns - 1)], RETURN).wait_recv()
        group(rs.at[0], RETURN).wait_send()
        group(rs.at[1, pl.ds(0, columns - 1)], RETURN + 1).wait_send()

    @pl.when(core == 0)
    def _():
        group(rr, RETURN).wait_recv()

    from_expert = one_hot(wide_piece & (spread(route_slot, wide_index) == wide_lane // PACK))
    total += dot(from_expert, rr[...].reshape(outer, -1))
    for i in range(tiles):
        cols = pl.ds(i * LANES, LANES)
        out_ref[:, cols] = tile_of(total, i)[:sessions]


def body(
    tokens,
    norm_scale_vector,
    router,
    routes,
    session_speaker,
    adapter_slots,
    speaker_down_weight,
    speaker_up_weight,
    routed_gate_weight,
    routed_up_weight,
    routed_down_weight,
    common_gate_weight,
    common_up_weight,
    common_down_weight,
):
    sessions, width = tokens.shape
    planes = lax.axis_size("dp") // 2
    columns = lax.axis_size("expert")
    half = common_gate_weight.shape[1]
    rank = speaker_down_weight.shape[2]
    hops = planes // 2
    tight = tight_tiles(width // LANES) * LANES
    vmem = pl.BlockSpec(memory_space=pltpu.VMEM)
    hbm = pl.BlockSpec(memory_space=pl.ANY)
    dma = pltpu.SemaphoreType.DMA
    packed = pltpu.VMEM((columns, 2 * PACK, 3 * LANES), BF)
    packed_two = pltpu.VMEM((2, columns, 2 * PACK, 3 * LANES), BF)
    over_z = pltpu.VMEM((planes, 2 * PACK, 3 * LANES), BF)
    wide_z = pltpu.VMEM((planes, 2 * PACK, 5 * LANES), BF)
    total = pl.pallas_call(
        functools.partial(block_kernel, planes, columns),
        out_shape=jax.ShapeDtypeStruct((sessions, width), F32),
        in_specs=[hbm] * 3 + [vmem] + [hbm] * 10,
        out_specs=vmem,
        scratch_shapes=[
            pltpu.SMEM((sessions,), I32),
            pltpu.SMEM((sessions,), I32),
            pltpu.SMEM(adapter_slots.shape, I32),
            pltpu.VMEM((width,), F32),
            pltpu.VMEM((columns, width), BF),
            dma((5,)),
            pltpu.VMEM((ROWS, width), F32),
            pltpu.VMEM((4, width, 2 * half), BF),
            pltpu.VMEM((4 * half, width), BF),
            pltpu.VMEM((2, rank, width), BF),
            pltpu.VMEM((2, rank, width), BF),
            packed,
            packed_two,
            over_z,
            over_z,
            wide_z,
            wide_z,
            packed_two,
            packed,
            wide_z,
            wide_z,
            pltpu.VMEM((2, PACK * ROWS, columns * 2 * PACK), BF),
            pltpu.VMEM((planes, 2 * ROWS, tight), BF),
            pltpu.VMEM((planes * ROWS, 4 * half), BF),
            pltpu.VMEM((planes, 2 * ROWS, tight), BF),
            pltpu.VMEM((2, 2 * ROWS, tight), BF),
            pltpu.VMEM((2, hops, 2 * ROWS, tight), BF),
            pltpu.VMEM((2, ROWS, tight), BF),
            dma((8,)),
            dma((2, 8)),
            dma((10,)),
            dma((10,)),
            dma((2, 2)),
            dma((2, hops, 2, 2)),
            dma((2, hops - 1)),
            dma((planes,)),
        ],
        compiler_params=pltpu.CompilerParams(
            collective_id=1, has_side_effects=True, vmem_limit_bytes=56 * 1024 * 1024
        ),
    )(
        routes,
        session_speaker,
        adapter_slots,
        tokens,
        norm_scale_vector,
        router.T,
        common_gate_weight[None],
        routed_gate_weight,
        common_up_weight[None],
        routed_up_weight,
        common_down_weight[None],
        routed_down_weight,
        speaker_down_weight,
        speaker_up_weight,
    )
    return (tokens.astype(F32) + total).astype(BF)


def solution(mesh):
    in_specs = (
        P(("dp", "expert"), None),
        P(),
        P(),
        P(("dp", "expert")),
        P(("dp", "expert")),
        P("expert", None),
        P("expert", "dp", None, None),
        P("expert", "dp", None, None),
        P("expert", None, "dp"),
        P("expert", None, "dp"),
        P("expert", "dp", None),
        P(None, "dp"),
        P(None, "dp"),
        P("dp", None),
    )
    out_specs = P(("dp", "expert"), None)
    return jax.shard_map(body, mesh=mesh, in_specs=in_specs, out_specs=out_specs, check_vma=False)
```

```python
import functools

import jax
import jax.numpy as jnp
from jax import lax
from jax.experimental import pallas as pl
from jax.experimental.pallas import tpu as pltpu
from jax.sharding import PartitionSpec as P

MESH = pl.DeviceIdType.MESH
BF = jnp.bfloat16
F32 = jnp.float32
I32 = jnp.int32
norm_eps = 1e-05
PARTS = 2
ROWS = 16
REAL = 13
LANES = 128
PACK = 8


def iota(shape, dim):
    return lax.broadcasted_iota(I32, shape, dim)


def one_hot(condition):
    return jnp.where(condition, 1.0, 0.0).astype(BF)


def stack(rows, fill):
    tiles = rows.shape[1] // LANES
    columns = []
    for t in range(-(-tiles // PACK)):
        pieces = []
        for j in range(PACK):
            i = t * PACK + j
            if i < tiles:
                pieces.append(rows[:, i * LANES : (i + 1) * LANES])
            else:
                pieces.append(jnp.full((ROWS, LANES), fill if i == tiles else 0.0, rows.dtype))
        columns.append(jnp.concatenate(pieces, axis=0))
    return jnp.concatenate(columns, axis=1)


def tile_of(stacked, i):
    t, j = i // PACK, i % PACK
    return stacked[j * ROWS : (j + 1) * ROWS, t * LANES : (t + 1) * LANES]


def unstack(stacked, tiles):
    return jnp.concatenate([tile_of(stacked, i) for i in range(tiles)], axis=1)


def tight_tiles(tiles):
    return next(n for n in range(tiles) if (tiles - n) <= ROWS - REAL and REAL <= n)


def moving(n, axis):
    shape = (n * ROWS, (ROWS - REAL) * ROWS)
    a, b = iota(shape[::-1], 1) if axis else iota(shape, 0), iota(shape[::-1], 0) if axis else iota(shape, 1)
    return one_hot((a // ROWS == jnp.bitwise_and(b, ROWS - 1)) & (jnp.bitwise_and(a, ROWS - 1) == REAL + b // ROWS))


def overflow_of(block, out_of):
    below = jnp.concatenate([block[:, i * LANES : (i + 1) * LANES] for i in range(REAL)], axis=0)
    return dot(out_of[...], below).astype(BF)


def tighten(overflow, n, into):
    placed = dot(into[...], overflow)
    return jnp.concatenate([placed[i * ROWS : (i + 1) * ROWS] for i in range(n)], axis=1)


def dot(a, b):
    return jnp.dot(a, b, preferred_element_type=F32)


def dot_t(a, b):
    return lax.dot_general(a, b, (((0,), (0,)), ((), ())), preferred_element_type=F32)


def dot_nt(a, b):
    return lax.dot_general(a, b, (((1,), (1,)), ((), ())), preferred_element_type=F32)


def block_kernel(
    planes,
    columns,
    routes_in,
    speaker_in,
    slots_in,
    tokens_ref,
    gain_in,
    router_in,
    cg_ref,
    rg_ref,
    cu_ref,
    ru_ref,
    cd_ref,
    rd_ref,
    down_ref,
    up_ref,
    out_ref,
    routes_ref,
    speaker_ref,
    slots_ref,
    gain_ref,
    router_ref,
    in_sem,
    tok,
    w1,
    w2,
    wd,
    wu,
    xs,
    xr,
    ls,
    ls2,
    ls4,
    lr,
    rs,
    rr,
    bs,
    br,
    pack_ref,
    gath,
    hid,
    pb,
    first,
    rb,
    yb,
    orders,
    into,
    out_of,
    own_sem,
    wsem,
    sent,
    got,
    exsem,
    ring_got,
    over_got,
    give_got,
):
    dp = lax.axis_index("dp")
    col = lax.axis_index("expert")
    z = dp // 2
    core = lax.rem(dp, 2)
    sessions, width = tokens_ref.shape
    tiles = width // LANES
    half = cg_ref.shape[2]
    hops = planes // 2
    tight = tight_tiles(tiles)
    left_out = tiles - tight
    cuts = [-(-tight * i // PARTS) * LANES for i in range(PARTS + 1)]
    sides = [pl.ds(a, b - a) for a, b in zip(cuts, cuts[1:])]
    sibling = (z * 2 + 1 - core, col)

    def plane(offset):
        return lax.rem(z + offset, planes)

    def remote(src, dst, send_sem, recv_sem, device):
        return pltpu.make_async_remote_copy(
            src, dst, send_sem, recv_sem, device_id=device, device_id_type=MESH
        )

    def group(view, index):
        return remote(view, view, sent.at[index], got.at[index], sibling)

    DISPATCH, RETURN, TO_ADAPTER, FROM_ADAPTER, GATHER, REDUCE, OVER, GIVE = 0, 2, 4, 5, 6, 7, 8, 9

    barrier = pltpu.get_barrier_semaphore()

    def greet(device):
        pl.semaphore_signal(barrier, inc=1, device_id=device, device_id_type=MESH)

    ring = 1
    while ring * ring < columns:
        ring += 1
    assert ring * ring == columns
    far_first = sorted(
        ((i, j) for i in range(ring) for j in range(ring)),
        key=lambda at: -sum(min(a, ring - a) for a in at),
    )

    def column(d):
        i, j = far_first[d]
        return lax.rem(col // ring + i, ring) * ring + lax.rem(lax.rem(col, ring) + j, ring)

    home = columns - 1
    near = ((plane(1) * 2 + core, col), (plane(planes - 1) * 2 + core, col))

    @pl.when(core == 1)
    def _():
        for device in near:
            greet(device)
        for d in range(home):
            greet((z * 2, column(d)))
            greet((z * 2 + 1, column(d)))
        greet(sibling)

    @pl.when(core == 0)
    def _():
        for d in range(1, planes):
            greet((plane(d) * 2, col))
        for d in range(columns):
            greet((z * 2 + 1, column(d)))

    fetched = (
        (routes_in, routes_ref),
        (speaker_in, speaker_ref),
        (slots_in, slots_ref),
        (gain_in, gain_ref),
        (router_in, router_ref),
    )
    fetches = [
        pltpu.make_async_copy(src, dst, in_sem.at[i]) for i, (src, dst) in enumerate(fetched)
    ]
    for copy in fetches:
        copy.start()
    for copy in fetches:
        copy.wait()

    tok[...] = jnp.zeros_like(tok)
    tok[0:sessions, :] = tokens_ref[...].astype(F32)
    x = tok[...]
    scale = lax.rsqrt(jnp.mean(x * x, axis=-1, keepdims=True) + norm_eps)
    normed = (x * scale * gain_ref[...][None, :]).astype(BF)

    routes = [routes_ref[s] for s in range(sessions)]
    route_slot = []
    for s in range(sessions):
        rank = jnp.int32(0)
        for earlier in range(s):
            rank = rank + jnp.where(routes[earlier] == routes[s], 1, 0)
        route_slot.append(routes[s] * 2 + rank)
    storage = [slots_ref[0, speaker_ref[s]] for s in range(sessions)]

    def spread(values, index):
        held = jnp.full(index.shape, -1, I32)
        for s in range(sessions):
            held = jnp.where(index == s, values[s], held)
        return held

    pairs = 2 * PACK
    outer = columns * pairs
    inner = PACK * ROWS
    row = iota((outer, inner), 0)
    lane = iota((outer, inner), 1)
    lane_session = jnp.bitwise_and(iota((1, inner), 1), ROWS - 1)
    same_piece = jnp.bitwise_and(row, PACK - 1) == lane // ROWS
    stacked = stack(normed, 1.0)
    to_expert = one_hot(same_piece & (row // PACK == spread(route_slot, lane_session)))
    xs[...] = dot(to_expert, stacked).astype(BF).reshape(xs.shape)
    to_adapter = one_hot(same_piece & (row // PACK == spread(storage, lane_session)))
    tail = stacked[: inner // 2, 2 * LANES :]
    tail = jnp.concatenate([tail, tail], axis=0)
    tail = jnp.where(iota(tail.shape, 0) // (inner // 2) == core, tail.astype(F32), 0.0).astype(BF)
    stacked = jnp.concatenate([stacked[:, : 2 * LANES], tail], axis=1)
    ls[...] = dot(to_adapter, stacked).astype(BF).reshape(ls.shape)

    def dispatch(d, source):
        return remote(
            xs.at[column(d)],
            xr.at[source, col],
            sent.at[DISPATCH + source],
            got.at[DISPATCH + source],
            (z * 2 + 1, column(d)),
        )

    def bring_back(d, h):
        return remote(
            rs.at[h, column(d)],
            rr.at[col],
            sent.at[RETURN + h],
            got.at[RETURN],
            (z * 2 + h, column(d)),
        )

    def over_planes(src, dst, index):
        sign = -1 if index == TO_ADAPTER else 1
        for d in sorted(range(1, planes), key=lambda d: sign * min(d, planes - d)):
            to = plane(d)
            remote(src.at[to], dst.at[z], sent.at[index], got.at[index], (to * 2, col)).start()

    slots_copy = remote(ls, ls2, exsem.at[0, 0], exsem.at[1, 0], sibling)
    adapter_copies = (
        remote(down_ref.at[0, 0], wd.at[1], wsem.at[0, 2], wsem.at[1, 2], sibling),
        remote(up_ref.at[0, 0], wu.at[1], wsem.at[0, 3], wsem.at[1, 3], sibling),
    )

    @pl.when(core == 1)
    def _():
        pl.semaphore_wait(barrier, 2 * columns + 1)
        slots_copy.start()
        for d in range(home):
            dispatch(d, 1).start()
        xr[1, col] = xs[col]

    @pl.when(core == 0)
    def _():
        pl.semaphore_wait(barrier, columns + planes - 1)
        for d in range(columns):
            dispatch(d, 0).start()

    @pl.when(core == 0)
    def _():
        slots_copy.wait_recv()
        ls4[:, :, 0 : 2 * LANES] = ls[:, :, 0 : 2 * LANES]
        ls4[:, :, 2 * LANES : 4 * LANES] = ls2[:, :, 0 : 2 * LANES]
        ls4[:, :, 4 * LANES :] = ls[:, :, 2 * LANES :] + ls2[:, :, 2 * LANES :]
        over_planes(ls4, lr, TO_ADAPTER)
        lr[z] = ls4[z]

    sources = (cg_ref, rg_ref, cu_ref, ru_ref)
    own = []
    for j in range(4):
        own.append(
            pltpu.make_async_copy(sources[j].at[0], w1.at[j, :, pl.ds(0, half)], own_sem.at[0])
        )
    for j, ref in enumerate((cd_ref, rd_ref)):
        own.append(
            pltpu.make_async_copy(ref.at[0], w2.at[pl.ds(2 * j * half, half)], own_sem.at[1])
        )
    for copy in own:
        copy.start()
    adapter = (
        pltpu.make_async_copy(down_ref.at[0, 0], wd.at[0], own_sem.at[2]),
        pltpu.make_async_copy(up_ref.at[0, 0], wu.at[0], own_sem.at[3]),
    )

    @pl.when(core == 0)
    def _():
        for copy in adapter:
            copy.start()

    shared = []
    for j in range(4):
        shared.append(
            remote(
                sources[j].at[0],
                w1.at[j, :, pl.ds(half, half)],
                wsem.at[0, 0],
                wsem.at[1, 0],
                sibling,
            )
        )
    for j, ref in enumerate((cd_ref, rd_ref)):
        shared.append(
            remote(
                ref.at[0],
                w2.at[pl.ds((2 * j + 1) * half, half)],
                wsem.at[0, 1],
                wsem.at[1, 1],
                sibling,
            )
        )
    for copy in shared:
        copy.start()

    @pl.when(core == 1)
    def _():
        for copy in adapter_copies:
            copy.start()

    wide_row = iota((inner, outer), 0)
    wide_lane = iota((inner, outer), 1)
    wide_piece = wide_row // ROWS == jnp.bitwise_and(wide_lane, PACK - 1)
    wide_index = jnp.bitwise_and(wide_row, ROWS - 1)

    slot_left = iota((outer, outer), 0) // PACK
    slot_right = iota((outer, outer), 1) // PACK
    orders[0] = one_hot(slot_left < slot_right)
    orders[1] = one_hot(slot_left == slot_right)
    into[...] = moving(tight, 0)
    out_of[...] = moving(REAL, 1)

    def close_up(h):
        arrived = xr[h].reshape(outer, 3 * LANES)
        flags = jnp.where(
            jnp.bitwise_and(row, PACK - 1) == tiles % PACK, arrived[:, 2 * LANES :], 0.0
        ).astype(BF)
        before = dot_t(flags, orders[0])
        taken = dot_t(flags, orders[1])
        pack_ref[h] = one_hot(
            wide_piece & (taken > 0.5) & (jnp.abs(before - wide_index.astype(F32)) < 0.5)
        )
        placed = dot(pack_ref[h], arrived)
        over = jnp.concatenate([tile_of(placed, tight + i) for i in range(left_out)], axis=0)
        gath[z, pl.ds(h * ROWS, ROWS), :] = (
            unstack(placed, tight) + tighten(over.astype(BF), tight, into)
        ).astype(BF)

    def pick(half_index):
        return one_hot(
            wide_piece
            & (wide_index == wide_lane // pairs)
            & (jnp.bitwise_and(wide_lane // PACK, 1) == half_index)
        )

    def adapter_apply():
        group(lr.at[pl.ds(0, planes - 1)], TO_ADAPTER).wait()
        for copy in adapter:
            copy.wait()
        for copy in adapter_copies:
            copy.wait_recv()
        back = jnp.zeros((outer, 5 * LANES), F32)
        for r in range(2):
            chosen = pick(r)
            got = dot(chosen, lr[...].reshape(outer, 5 * LANES)).astype(BF)
            parts = []
            for source in range(2):
                pieces = []
                for i in range(tiles):
                    t, j = i // PACK, i % PACK
                    if t == 2:
                        t, j = 4, j + 4 * source
                    else:
                        t = t + 2 * source
                    pieces.append(got[j * ROWS : (j + 1) * ROWS, t * LANES : (t + 1) * LANES])
                parts.append(jnp.concatenate(pieces, axis=1))
            low = dot_nt(jnp.concatenate(parts, axis=0), wd[r]).astype(BF)
            delta = dot(low, wu[r]).astype(BF)
            first_stack, second_stack = stack(delta[:ROWS], 0.0), stack(delta[ROWS:], 0.0)
            both = jnp.concatenate(
                [first_stack[: inner // 2, 2 * LANES :], second_stack[: inner // 2, 2 * LANES :]],
                axis=0,
            )
            back += dot_t(
                chosen,
                jnp.concatenate(
                    [first_stack[:, : 2 * LANES], second_stack[:, : 2 * LANES], both], axis=1
                ),
            )
        bs[...] = back.astype(BF).reshape(bs.shape)
        over_planes(bs, br, FROM_ADAPTER)
        br[z] = bs[z]

    reach = hops - 2
    middle = reach // 2
    inner_planes = [0]
    outer_planes = []
    for distance in range(1, reach + 1):
        both = [distance, planes - distance]
        if distance <= middle:
            inner_planes += both
        else:
            outer_planes = both + outer_planes
    given_planes = outer_planes + inner_planes[:0:-1] + [0]

    def length(d, part):
        return hops if part // (PARTS // 2) == d else hops - 1

    def from_plane(d, step):
        return plane(planes - step if d == 0 else step)

    def gather_copy(d, step, h, part):
        piece = gath.at[from_plane(d, step), pl.ds(h * ROWS, ROWS), sides[part]]
        return remote(piece, piece, sent.at[GATHER], ring_got.at[d, step, h, part], near[d])

    def hand_over(d, step):
        piece = gath.at[from_plane(d, step)]
        batch = 0 if step <= middle else 1
        return remote(piece, piece, sent.at[OVER], over_got.at[batch], sibling)

    def weights_here():
        gate_up, down = w1.at[:, :, pl.ds(0, half)], w2.at[pl.ds(0, 2 * half)]
        pltpu.make_async_copy(gate_up, gate_up, own_sem.at[0]).wait()
        pltpu.make_async_copy(down, down, own_sem.at[1]).wait()
        remote(gate_up, gate_up, wsem.at[0, 0], wsem.at[1, 0], sibling).wait()
        remote(down, down, wsem.at[0, 1], wsem.at[1, 1], sibling).wait()

    def apply_experts(offsets):
        blocks = []
        for o in offsets:
            for h in range(2):
                block = gath[plane(o), pl.ds(h * ROWS, ROWS), :]
                over = overflow_of(block, out_of)
                blocks.append(
                    jnp.concatenate(
                        [block] + [over[i * ROWS : (i + 1) * ROWS] for i in range(left_out)], axis=1
                    )
                )
        rows = jnp.concatenate(blocks, axis=0)
        logits = dot_nt(rows, router_ref[...])
        chosen = jnp.where(iota(logits.shape, 1) == col, logits, 0.0)
        gate_prob = 1.0 / (1.0 + jnp.exp(-jnp.sum(chosen, axis=1, keepdims=True)))
        held = pl.ds(0, len(offsets) * 2 * ROWS)
        holds = jnp.bitwise_and(iota((len(offsets) * 2 * ROWS, 1), 0), ROWS - 1) < REAL
        for n in range(2):
            gate = dot(rows, w1[n])
            value = gate / (1.0 + jnp.exp(-gate)) * dot(rows, w1[2 + n])
            if n == 1:
                value = value * gate_prob
            value = jnp.where(holds, value, 0.0)
            hid[held, pl.ds(2 * n * half, 2 * half)] = value.astype(BF)

        over = dot(hid[held, :], w2[:, tight * LANES :]).astype(BF)
        for i, o in enumerate(offsets):
            for h in range(2):
                k = (i * 2 + h) * ROWS
                pieces = [
                    over[k : k + ROWS, j * LANES : (j + 1) * LANES] for j in range(left_out)
                ]
                pb[plane(o), pl.ds(h * ROWS, ROWS), :] = tighten(
                    jnp.concatenate(pieces, axis=0), tight, into
                ).astype(BF)

        def add_columns(cols):
            product = dot(hid[held, :], w2[:, cols])
            for i, o in enumerate(offsets):
                k = i * 2 * ROWS
                pb[plane(o), :, cols] = (
                    product[k : k + 2 * ROWS] + pb[plane(o), :, cols].astype(F32)
                ).astype(BF)

        @pl.loop(0, tight // 2)
        def _(t):
            add_columns(pl.ds(pl.multiple_of(t * 2 * LANES, 2 * LANES), 2 * LANES))

        if tight % 2:
            add_columns(pl.ds((tight - 1) * LANES, LANES))

    def give(offset):
        dest = plane(offset)
        return remote(pb.at[dest], pb.at[dest], sent.at[GIVE], give_got.at[0 if offset in outer_planes else 1], sibling)

    def given_here(kind, batch):
        view = pb.at[pl.ds(0, len(kind))]
        remote(view, view, sent.at[GIVE], give_got.at[batch], sibling).wait_recv()

    def reduce_copy(d, step, h, part):
        place = (pl.ds(h * ROWS, ROWS), sides[part])
        src = first.at[(d, *place)] if step == 0 else rb.at[(d, step - 1, *place)]
        return remote(
            src,
            rb.at[(d, step, *place)],
            sent.at[REDUCE],
            ring_got.at[d, step, h, part],
            near[d],
        )

    def reduce_step(step, chain, given):
        for h in (0, 1):
            for part in range(PARTS):
                for d in range(2):
                    if length(d, part) == chain:
                        reduce_piece(step, chain, given, h, part, d)

    def reduce_piece(step, chain, given, h, part, d):
        place = (pl.ds(h * ROWS, ROWS), sides[part])
        offset = chain - step if d == 0 else planes - chain + step
        for batch, kind in enumerate((outer_planes, inner_planes)):
            if offset in kind and batch not in given:
                given_here(kind, batch)
                given.add(batch)
        dest = plane(offset)
        if step == 0:
            first[(d, *place)] = pb[(dest, *place)]
        else:
            reduce_copy(d, step - 1, h, part).wait_recv()
            rb[(d, step - 1, *place)] = (
                rb[(d, step - 1, *place)].astype(F32) + pb[(dest, *place)].astype(F32)
            ).astype(BF)
        reduce_copy(d, step, h, part).start()

    @pl.when(core == 1)
    def _():
        for h in (1, 0):
            group(xr.at[h, pl.ds(0, columns - h)], DISPATCH + h).wait_recv()
            close_up(h)
            for part in range(PARTS):
                for d in range(2):
                    gather_copy(d, 0, h, part).start()
        hand_over(0, 0).start()
        for step in range(1, hops + 1):
            if step == hops:
                weights_here()
                apply_experts([hops - 1, planes - hops + 1])
                reduce_step(0, hops - 1, set())
            for h in (1, 0):
                for part in range(PARTS):
                    for d in range(2):
                        if step > length(d, part):
                            continue
                        gather_copy(d, step - 1, h, part).wait_recv()
                        if step < length(d, part):
                            gather_copy(d, step, h, part).start()
            if step <= reach:
                for d in range(2):
                    hand_over(d, step).start()
        apply_experts([hops])
        reduce_step(0, hops, set())

    @pl.when(core == 0)
    def _():
        weights_here()
        inner_view = gath.at[pl.ds(0, len(inner_planes))]
        remote(inner_view, inner_view, sent.at[OVER], over_got.at[0], sibling).wait_recv()
        apply_experts(inner_planes)
        adapter_apply()
        outer_view = gath.at[pl.ds(0, len(outer_planes))]
        remote(outer_view, outer_view, sent.at[OVER], over_got.at[1], sibling).wait_recv()
        apply_experts(outer_planes)
        for offset in given_planes:
            give(offset).start()

    delta_copy = remote(br, br, exsem.at[0, 1], exsem.at[1, 1], sibling)

    @pl.when(core == 0)
    def _():
        group(br.at[pl.ds(0, planes - 1)], FROM_ADAPTER).wait()
        delta_copy.start()
        group(pb.at[pl.ds(0, len(given_planes))], GIVE).wait_send()
        delta_copy.wait_send()

    @pl.when(core == 1)
    def _():
        given = set()
        for step in range(1, hops):
            for chain in (hops - 1, hops):
                if step < chain:
                    reduce_step(step, chain, given)
        for h in (0, 1):
            for part in range(PARTS):
                cols = sides[part]
                rows = pl.ds(h * ROWS, ROWS)
                value = pb[z, rows, cols].astype(F32)
                for d in range(2):
                    last = length(d, part) - 1
                    reduce_copy(d, last, h, part).wait_recv()
                    value = value + rb[d, last, rows, cols].astype(F32)
                yb[h, :, cols] = value.astype(BF)
            result = yb[h]
            pieces = [result[:, i * LANES : (i + 1) * LANES] for i in range(tight)]
            over = overflow_of(result, out_of)
            pieces += [over[i * ROWS : (i + 1) * ROWS] for i in range(left_out)]
            result = stack(jnp.concatenate(pieces, axis=1), 0.0)
            rs[h] = dot_t(pack_ref[h], result).astype(BF).reshape(rs.shape[1:])
            for d in range(home):
                bring_back(d, h).start()
            if h == 0:
                bring_back(home, h).start()
            else:
                rr[col] = rs[h, col]

    @pl.when(core == 1)
    def _():
        slots_copy.wait_send()
        for copy in adapter_copies:
            copy.wait_send()
        group(gath.at[pl.ds(0, planes - 1)], GATHER).wait_send()
        group(gath.at[pl.ds(0, planes - 1)], REDUCE).wait_send()
        group(gath.at[pl.ds(0, 2 * reach + 1)], OVER).wait_send()
        group(xs.at[pl.ds(0, columns - 1)], DISPATCH + 1).wait_send()
        delta_copy.wait_recv()

    @pl.when(core == 0)
    def _():
        group(xs, DISPATCH).wait_send()

    stored = spread(storage, wide_index) == wide_lane // PACK
    body_part = br[:, :, pl.ds(pl.multiple_of(core * 2 * LANES, 2 * LANES), 2 * LANES)]
    tail_part = br[:, :, 4 * LANES :].reshape(outer, LANES)
    tail_piece = wide_row // ROWS + 4 * core == jnp.bitwise_and(wide_lane, PACK - 1)
    total = jnp.concatenate(
        [
            dot(one_hot(wide_piece & stored), body_part.reshape(outer, 2 * LANES)),
            dot(one_hot(tail_piece & stored), tail_part),
        ],
        axis=1,
    )
    @pl.when(core == 1)
    def _():
        group(rr.at[pl.ds(0, columns - 1)], RETURN).wait_recv()
        group(rs.at[0], RETURN).wait_send()
        group(rs.at[1, pl.ds(0, columns - 1)], RETURN + 1).wait_send()

    @pl.when(core == 0)
    def _():
        group(rr, RETURN).wait_recv()

    from_expert = one_hot(wide_piece & (spread(route_slot, wide_index) == wide_lane // PACK))
    total += dot(from_expert, rr[...].reshape(outer, -1))
    for i in range(tiles):
        cols = pl.ds(i * LANES, LANES)
        out_ref[:, cols] = tile_of(total, i)[:sessions]


def body(
    tokens,
    norm_scale_vector,
    router,
    routes,
    session_speaker,
    adapter_slots,
    speaker_down_weight,
    speaker_up_weight,
    routed_gate_weight,
    routed_up_weight,
    routed_down_weight,
    common_gate_weight,
    common_up_weight,
    common_down_weight,
):
    sessions, width = tokens.shape
    planes = lax.axis_size("dp") // 2
    columns = lax.axis_size("expert")
    half = common_gate_weight.shape[1]
    rank = speaker_down_weight.shape[2]
    hops = planes // 2
    tight = tight_tiles(width // LANES) * LANES
    vmem = pl.BlockSpec(memory_space=pltpu.VMEM)
    hbm = pl.BlockSpec(memory_space=pl.ANY)
    dma = pltpu.SemaphoreType.DMA
    packed = pltpu.VMEM((columns, 2 * PACK, 3 * LANES), BF)
    packed_two = pltpu.VMEM((2, columns, 2 * PACK, 3 * LANES), BF)
    over_z = pltpu.VMEM((planes, 2 * PACK, 3 * LANES), BF)
    wide_z = pltpu.VMEM((planes, 2 * PACK, 5 * LANES), BF)
    total = pl.pallas_call(
        functools.partial(block_kernel, planes, columns),
        out_shape=jax.ShapeDtypeStruct((sessions, width), F32),
        in_specs=[hbm] * 3 + [vmem] + [hbm] * 10,
        out_specs=vmem,
        scratch_shapes=[
            pltpu.SMEM((sessions,), I32),
            pltpu.SMEM((sessions,), I32),
            pltpu.SMEM(adapter_slots.shape, I32),
            pltpu.VMEM((width,), F32),
            pltpu.VMEM((columns, width), BF),
            dma((5,)),
            pltpu.VMEM((ROWS, width), F32),
            pltpu.VMEM((4, width, 2 * half), BF),
            pltpu.VMEM((4 * half, width), BF),
            pltpu.VMEM((2, rank, width), BF),
            pltpu.VMEM((2, rank, width), BF),
            packed,
            packed_two,
            over_z,
            over_z,
            wide_z,
            wide_z,
            packed_two,
            packed,
            wide_z,
            wide_z,
            pltpu.VMEM((2, PACK * ROWS, columns * 2 * PACK), BF),
            pltpu.VMEM((planes, 2 * ROWS, tight), BF),
            pltpu.VMEM((planes * ROWS, 4 * half), BF),
            pltpu.VMEM((planes, 2 * ROWS, tight), BF),
            pltpu.VMEM((2, 2 * ROWS, tight), BF),
            pltpu.VMEM((2, hops, 2 * ROWS, tight), BF),
            pltpu.VMEM((2, ROWS, tight), BF),
            pltpu.VMEM((2, columns * 2 * PACK, columns * 2 * PACK), BF),
            pltpu.VMEM((tight // LANES * ROWS, (ROWS - REAL) * ROWS), BF),
            pltpu.VMEM(((ROWS - REAL) * ROWS, REAL * ROWS), BF),
            dma((4,)),
            dma((2, 4)),
            dma((10,)),
            dma((10,)),
            dma((2, 2)),
            dma((2, hops, 2, PARTS)),
            dma((2,)),
            dma((2,)),
        ],
        compiler_params=pltpu.CompilerParams(
            collective_id=1, has_side_effects=True, vmem_limit_bytes=56 * 1024 * 1024
        ),
    )(
        routes,
        session_speaker,
        adapter_slots,
        tokens,
        norm_scale_vector,
        router.T,
        common_gate_weight[None],
        routed_gate_weight,
        common_up_weight[None],
        routed_up_weight,
        common_down_weight[None],
        routed_down_weight,
        speaker_down_weight,
        speaker_up_weight,
    )
    return (tokens.astype(F32) + total).astype(BF)


def solution(mesh):
    in_specs = (
        P(("dp", "expert"), None),
        P(),
        P(),
        P(("dp", "expert")),
        P(("dp", "expert")),
        P("expert", None),
        P("expert", "dp", None, None),
        P("expert", "dp", None, None),
        P("expert", None, "dp"),
        P("expert", None, "dp"),
        P("expert", "dp", None),
        P(None, "dp"),
        P(None, "dp"),
        P("dp", None),
    )
    out_specs = P(("dp", "expert"), None)
    return jax.shard_map(body, mesh=mesh, in_specs=in_specs, out_specs=out_specs, check_vma=False)
```

```python
import functools

import jax
import jax.numpy as jnp
from jax import lax
from jax.experimental import pallas as pl
from jax.experimental.pallas import tpu as pltpu
from jax.sharding import PartitionSpec as P

MESH = pl.DeviceIdType.MESH
BF = jnp.bfloat16
F32 = jnp.float32
I32 = jnp.int32
norm_eps = 1e-05
PARTS = 2
ROWS = 16
REAL = 13
LANES = 128
PACK = 8


def iota(shape, dim):
    return lax.broadcasted_iota(I32, shape, dim)


def one_hot(condition):
    return jnp.where(condition, 1.0, 0.0).astype(BF)


def stack(rows, fill):
    tiles = rows.shape[1] // LANES
    columns = []
    for t in range(-(-tiles // PACK)):
        pieces = []
        for j in range(PACK):
            i = t * PACK + j
            if i < tiles:
                pieces.append(rows[:, i * LANES : (i + 1) * LANES])
            else:
                pieces.append(jnp.full((ROWS, LANES), fill if i == tiles else 0.0, rows.dtype))
        columns.append(jnp.concatenate(pieces, axis=0))
    return jnp.concatenate(columns, axis=1)


def tile_of(stacked, i):
    t, j = i // PACK, i % PACK
    return stacked[j * ROWS : (j + 1) * ROWS, t * LANES : (t + 1) * LANES]


def unstack(stacked, tiles):
    return jnp.concatenate([tile_of(stacked, i) for i in range(tiles)], axis=1)


def tight_tiles(tiles):
    return next(n for n in range(tiles) if (tiles - n) <= ROWS - REAL and REAL <= n)


def moving(n, axis):
    shape = (n * ROWS, (ROWS - REAL) * ROWS)
    a, b = iota(shape[::-1], 1) if axis else iota(shape, 0), iota(shape[::-1], 0) if axis else iota(shape, 1)
    return one_hot((a // ROWS == jnp.bitwise_and(b, ROWS - 1)) & (jnp.bitwise_and(a, ROWS - 1) == REAL + b // ROWS))


def overflow_of(block, out_of):
    below = jnp.concatenate([block[:, i * LANES : (i + 1) * LANES] for i in range(REAL)], axis=0)
    return dot(out_of[...], below).astype(BF)


def tighten(overflow, n, into):
    placed = dot(into[...], overflow)
    return jnp.concatenate([placed[i * ROWS : (i + 1) * ROWS] for i in range(n)], axis=1)


def dot(a, b):
    return jnp.dot(a, b, preferred_element_type=F32)


def dot_t(a, b):
    return lax.dot_general(a, b, (((0,), (0,)), ((), ())), preferred_element_type=F32)


def dot_nt(a, b):
    return lax.dot_general(a, b, (((1,), (1,)), ((), ())), preferred_element_type=F32)


def block_kernel(
    planes,
    columns,
    routes_in,
    speaker_in,
    slots_in,
    tokens_ref,
    gain_in,
    router_in,
    cg_ref,
    rg_ref,
    cu_ref,
    ru_ref,
    cd_ref,
    rd_ref,
    down_ref,
    up_ref,
    out_ref,
    routes_ref,
    speaker_ref,
    slots_ref,
    gain_ref,
    router_ref,
    in_sem,
    tok,
    w1,
    w2,
    wd,
    wu,
    xs,
    xr,
    ls,
    ls2,
    ls4,
    lr,
    rs,
    rr,
    bs,
    br,
    pack_ref,
    gath,
    hid,
    pb,
    first,
    rb,
    yb,
    orders,
    into,
    out_of,
    own_sem,
    wsem,
    sent,
    got,
    exsem,
    ring_got,
    over_got,
    give_got,
):
    dp = lax.axis_index("dp")
    col = lax.axis_index("expert")
    z = dp // 2
    core = lax.rem(dp, 2)
    sessions, width = tokens_ref.shape
    tiles = width // LANES
    half = cg_ref.shape[2]
    hops = planes // 2
    tight = tight_tiles(tiles)
    left_out = tiles - tight
    cuts = [-(-tight * i // PARTS) * LANES for i in range(PARTS + 1)]
    sides = [pl.ds(a, b - a) for a, b in zip(cuts, cuts[1:])]
    sibling = (z * 2 + 1 - core, col)

    def plane(offset):
        return lax.rem(z + offset, planes)

    def remote(src, dst, send_sem, recv_sem, device):
        return pltpu.make_async_remote_copy(
            src, dst, send_sem, recv_sem, device_id=device, device_id_type=MESH
        )

    def group(view, index):
        return remote(view, view, sent.at[index], got.at[index], sibling)

    DISPATCH, RETURN, TO_ADAPTER, FROM_ADAPTER, GATHER, REDUCE, OVER, GIVE = 0, 2, 4, 5, 6, 7, 8, 9

    barrier = pltpu.get_barrier_semaphore()

    def greet(device):
        pl.semaphore_signal(barrier, inc=1, device_id=device, device_id_type=MESH)

    ring = 1
    while ring * ring < columns:
        ring += 1
    assert ring * ring == columns
    far_first = sorted(
        ((i, j) for i in range(ring) for j in range(ring)),
        key=lambda at: -sum(min(a, ring - a) for a in at),
    )

    def column(d):
        i, j = far_first[d]
        return lax.rem(col // ring + i, ring) * ring + lax.rem(lax.rem(col, ring) + j, ring)

    home = columns - 1
    near = ((plane(1) * 2 + core, col), (plane(planes - 1) * 2 + core, col))
    next_but_one = ((plane(2) * 2 + core, col), (plane(planes - 2) * 2 + core, col))

    @pl.when(core == 1)
    def _():
        for device in near + next_but_one:
            greet(device)
        for d in range(home):
            greet((z * 2, column(d)))
            greet((z * 2 + 1, column(d)))
        greet(sibling)

    @pl.when(core == 0)
    def _():
        for d in range(1, planes):
            greet((plane(d) * 2, col))
        for d in range(columns):
            greet((z * 2 + 1, column(d)))

    fetched = (
        (routes_in, routes_ref),
        (speaker_in, speaker_ref),
        (slots_in, slots_ref),
        (gain_in, gain_ref),
        (router_in, router_ref),
    )
    fetches = [
        pltpu.make_async_copy(src, dst, in_sem.at[i]) for i, (src, dst) in enumerate(fetched)
    ]
    for copy in fetches:
        copy.start()
    for copy in fetches:
        copy.wait()

    tok[...] = jnp.zeros_like(tok)
    tok[0:sessions, :] = tokens_ref[...].astype(F32)
    x = tok[...]
    scale = lax.rsqrt(jnp.mean(x * x, axis=-1, keepdims=True) + norm_eps)
    normed = (x * scale * gain_ref[...][None, :]).astype(BF)

    routes = [routes_ref[s] for s in range(sessions)]
    route_slot = []
    for s in range(sessions):
        rank = jnp.int32(0)
        for earlier in range(s):
            rank = rank + jnp.where(routes[earlier] == routes[s], 1, 0)
        route_slot.append(routes[s] * 2 + rank)
    storage = [slots_ref[0, speaker_ref[s]] for s in range(sessions)]

    def spread(values, index):
        held = jnp.full(index.shape, -1, I32)
        for s in range(sessions):
            held = jnp.where(index == s, values[s], held)
        return held

    pairs = 2 * PACK
    outer = columns * pairs
    inner = PACK * ROWS
    row = iota((outer, inner), 0)
    lane = iota((outer, inner), 1)
    lane_session = jnp.bitwise_and(iota((1, inner), 1), ROWS - 1)
    same_piece = jnp.bitwise_and(row, PACK - 1) == lane // ROWS
    stacked = stack(normed, 1.0)
    to_expert = one_hot(same_piece & (row // PACK == spread(route_slot, lane_session)))
    xs[...] = dot(to_expert, stacked).astype(BF).reshape(xs.shape)
    to_adapter = one_hot(same_piece & (row // PACK == spread(storage, lane_session)))
    tail = stacked[: inner // 2, 2 * LANES :]
    tail = jnp.concatenate([tail, tail], axis=0)
    tail = jnp.where(iota(tail.shape, 0) // (inner // 2) == core, tail.astype(F32), 0.0).astype(BF)
    stacked = jnp.concatenate([stacked[:, : 2 * LANES], tail], axis=1)
    ls[...] = dot(to_adapter, stacked).astype(BF).reshape(ls.shape)

    def dispatch(d, source):
        return remote(
            xs.at[column(d)],
            xr.at[source, col],
            sent.at[DISPATCH + source],
            got.at[DISPATCH + source],
            (z * 2 + 1, column(d)),
        )

    def bring_back(d, h):
        return remote(
            rs.at[h, column(d)],
            rr.at[col],
            sent.at[RETURN + h],
            got.at[RETURN],
            (z * 2 + h, column(d)),
        )

    def over_planes(src, dst, index):
        sign = -1 if index == TO_ADAPTER else 1
        for d in sorted(range(1, planes), key=lambda d: sign * min(d, planes - d)):
            to = plane(d)
            remote(src.at[to], dst.at[z], sent.at[index], got.at[index], (to * 2, col)).start()

    slots_copy = remote(ls, ls2, exsem.at[0, 0], exsem.at[1, 0], sibling)
    adapter_copies = (
        remote(down_ref.at[0, 0], wd.at[1], wsem.at[0, 2], wsem.at[1, 2], sibling),
        remote(up_ref.at[0, 0], wu.at[1], wsem.at[0, 3], wsem.at[1, 3], sibling),
    )

    @pl.when(core == 1)
    def _():
        pl.semaphore_wait(barrier, 2 * columns + 3)
        slots_copy.start()
        for d in range(home):
            dispatch(d, 1).start()
        xr[1, col] = xs[col]

    @pl.when(core == 0)
    def _():
        pl.semaphore_wait(barrier, columns + planes - 1)
        for d in range(columns):
            dispatch(d, 0).start()

    @pl.when(core == 0)
    def _():
        slots_copy.wait_recv()
        ls4[:, :, 0 : 2 * LANES] = ls[:, :, 0 : 2 * LANES]
        ls4[:, :, 2 * LANES : 4 * LANES] = ls2[:, :, 0 : 2 * LANES]
        ls4[:, :, 4 * LANES :] = ls[:, :, 2 * LANES :] + ls2[:, :, 2 * LANES :]
        over_planes(ls4, lr, TO_ADAPTER)
        lr[z] = ls4[z]

    sources = (cg_ref, rg_ref, cu_ref, ru_ref)
    own = []
    for j in range(4):
        own.append(
            pltpu.make_async_copy(sources[j].at[0], w1.at[j, :, pl.ds(0, half)], own_sem.at[0])
        )
    for j, ref in enumerate((cd_ref, rd_ref)):
        own.append(
            pltpu.make_async_copy(ref.at[0], w2.at[pl.ds(2 * j * half, half)], own_sem.at[1])
        )
    for copy in own:
        copy.start()
    adapter = (
        pltpu.make_async_copy(down_ref.at[0, 0], wd.at[0], own_sem.at[2]),
        pltpu.make_async_copy(up_ref.at[0, 0], wu.at[0], own_sem.at[3]),
    )

    @pl.when(core == 0)
    def _():
        for copy in adapter:
            copy.start()

    shared = []
    for j in range(4):
        shared.append(
            remote(
                sources[j].at[0],
                w1.at[j, :, pl.ds(half, half)],
                wsem.at[0, 0],
                wsem.at[1, 0],
                sibling,
            )
        )
    for j, ref in enumerate((cd_ref, rd_ref)):
        shared.append(
            remote(
                ref.at[0],
                w2.at[pl.ds((2 * j + 1) * half, half)],
                wsem.at[0, 1],
                wsem.at[1, 1],
                sibling,
            )
        )
    for copy in shared:
        copy.start()

    @pl.when(core == 1)
    def _():
        for copy in adapter_copies:
            copy.start()

    wide_row = iota((inner, outer), 0)
    wide_lane = iota((inner, outer), 1)
    wide_piece = wide_row // ROWS == jnp.bitwise_and(wide_lane, PACK - 1)
    wide_index = jnp.bitwise_and(wide_row, ROWS - 1)

    slot_left = iota((outer, outer), 0) // PACK
    slot_right = iota((outer, outer), 1) // PACK
    orders[0] = one_hot(slot_left < slot_right)
    orders[1] = one_hot(slot_left == slot_right)
    into[...] = moving(tight, 0)
    out_of[...] = moving(REAL, 1)

    def close_up(h):
        arrived = xr[h].reshape(outer, 3 * LANES)
        flags = jnp.where(
            jnp.bitwise_and(row, PACK - 1) == tiles % PACK, arrived[:, 2 * LANES :], 0.0
        ).astype(BF)
        before = dot_t(flags, orders[0])
        taken = dot_t(flags, orders[1])
        pack_ref[h] = one_hot(
            wide_piece & (taken > 0.5) & (jnp.abs(before - wide_index.astype(F32)) < 0.5)
        )
        placed = dot(pack_ref[h], arrived)
        over = jnp.concatenate([tile_of(placed, tight + i) for i in range(left_out)], axis=0)
        gath[z, pl.ds(h * ROWS, ROWS), :] = (
            unstack(placed, tight) + tighten(over.astype(BF), tight, into)
        ).astype(BF)

    def pick(half_index):
        return one_hot(
            wide_piece
            & (wide_index == wide_lane // pairs)
            & (jnp.bitwise_and(wide_lane // PACK, 1) == half_index)
        )

    def adapter_apply():
        group(lr.at[pl.ds(0, planes - 1)], TO_ADAPTER).wait()
        for copy in adapter:
            copy.wait()
        for copy in adapter_copies:
            copy.wait_recv()
        back = jnp.zeros((outer, 5 * LANES), F32)
        for r in range(2):
            chosen = pick(r)
            got = dot(chosen, lr[...].reshape(outer, 5 * LANES)).astype(BF)
            parts = []
            for source in range(2):
                pieces = []
                for i in range(tiles):
                    t, j = i // PACK, i % PACK
                    if t == 2:
                        t, j = 4, j + 4 * source
                    else:
                        t = t + 2 * source
                    pieces.append(got[j * ROWS : (j + 1) * ROWS, t * LANES : (t + 1) * LANES])
                parts.append(jnp.concatenate(pieces, axis=1))
            low = dot_nt(jnp.concatenate(parts, axis=0), wd[r]).astype(BF)
            delta = dot(low, wu[r]).astype(BF)
            first_stack, second_stack = stack(delta[:ROWS], 0.0), stack(delta[ROWS:], 0.0)
            both = jnp.concatenate(
                [first_stack[: inner // 2, 2 * LANES :], second_stack[: inner // 2, 2 * LANES :]],
                axis=0,
            )
            back += dot_t(
                chosen,
                jnp.concatenate(
                    [first_stack[:, : 2 * LANES], second_stack[:, : 2 * LANES], both], axis=1
                ),
            )
        bs[...] = back.astype(BF).reshape(bs.shape)
        over_planes(bs, br, FROM_ADAPTER)
        br[z] = bs[z]

    reach = hops - 2
    middle = reach // 2
    inner_planes = [0]
    outer_planes = []
    for distance in range(1, reach + 1):
        both = [distance, planes - distance]
        if distance <= middle:
            inner_planes += both
        else:
            outer_planes = both + outer_planes
    given_planes = outer_planes + inner_planes[:0:-1] + [0]

    def length(d, part):
        return hops if part // (PARTS // 2) == d else hops - 1

    def from_plane(d, step):
        return plane(planes - step if d == 0 else step)

    def gather_copy(d, step, h, part):
        piece = gath.at[from_plane(d, step), pl.ds(h * ROWS, ROWS), sides[part]]
        return remote(piece, piece, sent.at[GATHER], ring_got.at[d, step, h, part], near[d])

    def gather_skip(d, h, part):
        piece = gath.at[from_plane(d, hops - 2), pl.ds(h * ROWS, ROWS), sides[part]]
        got_at = ring_got.at[d, hops - 1, h, part]
        return remote(piece, piece, sent.at[GATHER], got_at, next_but_one[d])

    def hand_over(d, step):
        piece = gath.at[from_plane(d, step)]
        batch = 0 if step <= middle else 1
        return remote(piece, piece, sent.at[OVER], over_got.at[batch], sibling)

    def weights_here():
        gate_up, down = w1.at[:, :, pl.ds(0, half)], w2.at[pl.ds(0, 2 * half)]
        pltpu.make_async_copy(gate_up, gate_up, own_sem.at[0]).wait()
        pltpu.make_async_copy(down, down, own_sem.at[1]).wait()
        remote(gate_up, gate_up, wsem.at[0, 0], wsem.at[1, 0], sibling).wait()
        remote(down, down, wsem.at[0, 1], wsem.at[1, 1], sibling).wait()

    def apply_experts(offsets):
        blocks = []
        for o in offsets:
            for h in range(2):
                block = gath[plane(o), pl.ds(h * ROWS, ROWS), :]
                over = overflow_of(block, out_of)
                blocks.append(
                    jnp.concatenate(
                        [block] + [over[i * ROWS : (i + 1) * ROWS] for i in range(left_out)], axis=1
                    )
                )
        rows = jnp.concatenate(blocks, axis=0)
        logits = dot_nt(rows, router_ref[...])
        chosen = jnp.where(iota(logits.shape, 1) == col, logits, 0.0)
        gate_prob = 1.0 / (1.0 + jnp.exp(-jnp.sum(chosen, axis=1, keepdims=True)))
        held = pl.ds(0, len(offsets) * 2 * ROWS)
        holds = jnp.bitwise_and(iota((len(offsets) * 2 * ROWS, 1), 0), ROWS - 1) < REAL
        for n in range(2):
            gate = dot(rows, w1[n])
            value = gate / (1.0 + jnp.exp(-gate)) * dot(rows, w1[2 + n])
            if n == 1:
                value = value * gate_prob
            value = jnp.where(holds, value, 0.0)
            hid[held, pl.ds(2 * n * half, 2 * half)] = value.astype(BF)

        over = dot(hid[held, :], w2[:, tight * LANES :]).astype(BF)
        for i, o in enumerate(offsets):
            for h in range(2):
                k = (i * 2 + h) * ROWS
                pieces = [
                    over[k : k + ROWS, j * LANES : (j + 1) * LANES] for j in range(left_out)
                ]
                pb[plane(o), pl.ds(h * ROWS, ROWS), :] = tighten(
                    jnp.concatenate(pieces, axis=0), tight, into
                ).astype(BF)

        def add_columns(cols):
            product = dot(hid[held, :], w2[:, cols])
            for i, o in enumerate(offsets):
                k = i * 2 * ROWS
                pb[plane(o), :, cols] = (
                    product[k : k + 2 * ROWS] + pb[plane(o), :, cols].astype(F32)
                ).astype(BF)

        @pl.loop(0, tight // 2)
        def _(t):
            add_columns(pl.ds(pl.multiple_of(t * 2 * LANES, 2 * LANES), 2 * LANES))

        if tight % 2:
            add_columns(pl.ds((tight - 1) * LANES, LANES))

    def give(offset):
        dest = plane(offset)
        return remote(pb.at[dest], pb.at[dest], sent.at[GIVE], give_got.at[0 if offset in outer_planes else 1], sibling)

    def given_here(kind, batch):
        view = pb.at[pl.ds(0, len(kind))]
        remote(view, view, sent.at[GIVE], give_got.at[batch], sibling).wait_recv()

    def reduce_copy(d, step, h, part):
        place = (pl.ds(h * ROWS, ROWS), sides[part])
        device = near[d]
        if step == 0:
            src = first.at[(d, *place)]
            if length(d, part) == hops:
                device = next_but_one[d]
        elif step == 1 and length(d, part) == hops:
            src = pb.at[(plane(hops - 1 if d == 0 else planes - hops + 1), *place)]
        else:
            src = rb.at[(d, step - 1, *place)]
        return remote(
            src,
            rb.at[(d, step, *place)],
            sent.at[REDUCE],
            ring_got.at[d, step, h, part],
            device,
        )

    def reduce_step(step, chain, given):
        for h in (0, 1):
            for part in range(PARTS):
                for d in range(2):
                    if length(d, part) == chain:
                        reduce_piece(step, chain, given, h, part, d)

    def reduce_piece(step, chain, given, h, part, d):
        place = (pl.ds(h * ROWS, ROWS), sides[part])
        offset = chain - step if d == 0 else planes - chain + step
        for batch, kind in enumerate((outer_planes, inner_planes)):
            if offset in kind and batch not in given:
                given_here(kind, batch)
                given.add(batch)
        dest = plane(offset)
        if step == 0:
            first[(d, *place)] = pb[(dest, *place)]
        elif step > 1 or chain < hops:
            value = pb[(dest, *place)].astype(F32)
            if step == 2 and chain == hops:
                reduce_copy(d, 0, h, part).wait_recv()
                value = value + rb[(d, 0, *place)].astype(F32)
            reduce_copy(d, step - 1, h, part).wait_recv()
            rb[(d, step - 1, *place)] = (rb[(d, step - 1, *place)].astype(F32) + value).astype(BF)
        reduce_copy(d, step, h, part).start()

    @pl.when(core == 1)
    def _():
        for h in (1, 0):
            group(xr.at[h, pl.ds(0, columns - h)], DISPATCH + h).wait_recv()
            close_up(h)
            for part in range(PARTS):
                for d in range(2):
                    gather_copy(d, 0, h, part).start()
        hand_over(0, 0).start()
        for step in range(1, hops + 1):
            if step == hops:
                weights_here()
                apply_experts([hops - 1, planes - hops + 1])
                reduce_step(0, hops - 1, set())
                reduce_step(1, hops, set())
            for h in (1, 0):
                for part in range(PARTS):
                    for d in range(2):
                        if step > length(d, part):
                            continue
                        gather_copy(d, step - 1, h, part).wait_recv()
                        if step < hops - 1:
                            gather_copy(d, step, h, part).start()
                        if step == hops - 2 and length(d, part) == hops:
                            gather_skip(d, h, part).start()
            if step <= reach:
                for d in range(2):
                    hand_over(d, step).start()
        apply_experts([hops])
        reduce_step(0, hops, set())

    @pl.when(core == 0)
    def _():
        weights_here()
        inner_view = gath.at[pl.ds(0, len(inner_planes))]
        remote(inner_view, inner_view, sent.at[OVER], over_got.at[0], sibling).wait_recv()
        apply_experts(inner_planes)
        adapter_apply()
        outer_view = gath.at[pl.ds(0, len(outer_planes))]
        remote(outer_view, outer_view, sent.at[OVER], over_got.at[1], sibling).wait_recv()
        apply_experts(outer_planes)
        for offset in given_planes:
            give(offset).start()

    delta_copy = remote(br, br, exsem.at[0, 1], exsem.at[1, 1], sibling)

    @pl.when(core == 0)
    def _():
        group(br.at[pl.ds(0, planes - 1)], FROM_ADAPTER).wait()
        delta_copy.start()
        group(pb.at[pl.ds(0, len(given_planes))], GIVE).wait_send()
        delta_copy.wait_send()

    @pl.when(core == 1)
    def _():
        given = set()
        for step in range(1, hops):
            for chain in (hops - 1, hops):
                if step < chain and (step, chain) != (1, hops):
                    reduce_step(step, chain, given)
        for h in (0, 1):
            for part in range(PARTS):
                cols = sides[part]
                rows = pl.ds(h * ROWS, ROWS)
                value = pb[z, rows, cols].astype(F32)
                for d in range(2):
                    last = length(d, part) - 1
                    reduce_copy(d, last, h, part).wait_recv()
                    value = value + rb[d, last, rows, cols].astype(F32)
                yb[h, :, cols] = value.astype(BF)
            result = yb[h]
            pieces = [result[:, i * LANES : (i + 1) * LANES] for i in range(tight)]
            over = overflow_of(result, out_of)
            pieces += [over[i * ROWS : (i + 1) * ROWS] for i in range(left_out)]
            result = stack(jnp.concatenate(pieces, axis=1), 0.0)
            rs[h] = dot_t(pack_ref[h], result).astype(BF).reshape(rs.shape[1:])
            for d in range(home):
                bring_back(d, h).start()
            if h == 0:
                bring_back(home, h).start()
            else:
                rr[col] = rs[h, col]

    @pl.when(core == 1)
    def _():
        slots_copy.wait_send()
        for copy in adapter_copies:
            copy.wait_send()
        group(gath.at[pl.ds(0, planes - 1)], GATHER).wait_send()
        group(gath.at[pl.ds(0, planes - 1)], REDUCE).wait_send()
        group(gath.at[pl.ds(0, 2 * reach + 1)], OVER).wait_send()
        group(xs.at[pl.ds(0, columns - 1)], DISPATCH + 1).wait_send()
        delta_copy.wait_recv()

    @pl.when(core == 0)
    def _():
        group(xs, DISPATCH).wait_send()

    stored = spread(storage, wide_index) == wide_lane // PACK
    body_part = br[:, :, pl.ds(pl.multiple_of(core * 2 * LANES, 2 * LANES), 2 * LANES)]
    tail_part = br[:, :, 4 * LANES :].reshape(outer, LANES)
    tail_piece = wide_row // ROWS + 4 * core == jnp.bitwise_and(wide_lane, PACK - 1)
    total = jnp.concatenate(
        [
            dot(one_hot(wide_piece & stored), body_part.reshape(outer, 2 * LANES)),
            dot(one_hot(tail_piece & stored), tail_part),
        ],
        axis=1,
    )
    @pl.when(core == 1)
    def _():
        group(rr.at[pl.ds(0, columns - 1)], RETURN).wait_recv()
        group(rs.at[0], RETURN).wait_send()
        group(rs.at[1, pl.ds(0, columns - 1)], RETURN + 1).wait_send()

    @pl.when(core == 0)
    def _():
        group(rr, RETURN).wait_recv()

    from_expert = one_hot(wide_piece & (spread(route_slot, wide_index) == wide_lane // PACK))
    total += dot(from_expert, rr[...].reshape(outer, -1))
    for i in range(tiles):
        cols = pl.ds(i * LANES, LANES)
        out_ref[:, cols] = (tok[:, cols] + tile_of(total, i))[:sessions].astype(BF)


def body(
    tokens,
    norm_scale_vector,
    router,
    routes,
    session_speaker,
    adapter_slots,
    speaker_down_weight,
    speaker_up_weight,
    routed_gate_weight,
    routed_up_weight,
    routed_down_weight,
    common_gate_weight,
    common_up_weight,
    common_down_weight,
):
    sessions, width = tokens.shape
    planes = lax.axis_size("dp") // 2
    columns = lax.axis_size("expert")
    half = common_gate_weight.shape[1]
    rank = speaker_down_weight.shape[2]
    hops = planes // 2
    tight = tight_tiles(width // LANES) * LANES
    vmem = pl.BlockSpec(memory_space=pltpu.VMEM)
    hbm = pl.BlockSpec(memory_space=pl.ANY)
    dma = pltpu.SemaphoreType.DMA
    packed = pltpu.VMEM((columns, 2 * PACK, 3 * LANES), BF)
    packed_two = pltpu.VMEM((2, columns, 2 * PACK, 3 * LANES), BF)
    over_z = pltpu.VMEM((planes, 2 * PACK, 3 * LANES), BF)
    wide_z = pltpu.VMEM((planes, 2 * PACK, 5 * LANES), BF)
    return pl.pallas_call(
        functools.partial(block_kernel, planes, columns),
        out_shape=jax.ShapeDtypeStruct((sessions, width), BF),
        in_specs=[hbm] * 3 + [vmem] + [hbm] * 10,
        out_specs=vmem,
        scratch_shapes=[
            pltpu.SMEM((sessions,), I32),
            pltpu.SMEM((sessions,), I32),
            pltpu.SMEM(adapter_slots.shape, I32),
            pltpu.VMEM((width,), F32),
            pltpu.VMEM((columns, width), BF),
            dma((5,)),
            pltpu.VMEM((ROWS, width), F32),
            pltpu.VMEM((4, width, 2 * half), BF),
            pltpu.VMEM((4 * half, width), BF),
            pltpu.VMEM((2, rank, width), BF),
            pltpu.VMEM((2, rank, width), BF),
            packed,
            packed_two,
            over_z,
            over_z,
            wide_z,
            wide_z,
            packed_two,
            packed,
            wide_z,
            wide_z,
            pltpu.VMEM((2, PACK * ROWS, columns * 2 * PACK), BF),
            pltpu.VMEM((planes, 2 * ROWS, tight), BF),
            pltpu.VMEM((planes * ROWS, 4 * half), BF),
            pltpu.VMEM((planes, 2 * ROWS, tight), BF),
            pltpu.VMEM((2, 2 * ROWS, tight), BF),
            pltpu.VMEM((2, hops, 2 * ROWS, tight), BF),
            pltpu.VMEM((2, ROWS, tight), BF),
            pltpu.VMEM((2, columns * 2 * PACK, columns * 2 * PACK), BF),
            pltpu.VMEM((tight // LANES * ROWS, (ROWS - REAL) * ROWS), BF),
            pltpu.VMEM(((ROWS - REAL) * ROWS, REAL * ROWS), BF),
            dma((4,)),
            dma((2, 4)),
            dma((10,)),
            dma((10,)),
            dma((2, 2)),
            dma((2, hops, 2, PARTS)),
            dma((2,)),
            dma((2,)),
        ],
        compiler_params=pltpu.CompilerParams(
            collective_id=1, has_side_effects=True, vmem_limit_bytes=56 * 1024 * 1024
        ),
    )(
        routes,
        session_speaker,
        adapter_slots,
        tokens,
        norm_scale_vector,
        router.T,
        common_gate_weight[None],
        routed_gate_weight,
        common_up_weight[None],
        routed_up_weight,
        common_down_weight[None],
        routed_down_weight,
        speaker_down_weight,
        speaker_up_weight,
    )


def solution(mesh):
    in_specs = (
        P(("dp", "expert"), None),
        P(),
        P(),
        P(("dp", "expert")),
        P(("dp", "expert")),
        P("expert", None),
        P("expert", "dp", None, None),
        P("expert", "dp", None, None),
        P("expert", None, "dp"),
        P("expert", None, "dp"),
        P("expert", "dp", None),
        P(None, "dp"),
        P(None, "dp"),
        P("dp", None),
    )
    out_specs = P(("dp", "expert"), None)
    return jax.shard_map(body, mesh=mesh, in_specs=in_specs, out_specs=out_specs, check_vma=False)
```
